512 devices in a mesh: dp: 32 (over x_lo, z), cls: 16 (over x_hi, y, core).
Axes of the slice: x: 4 (x_hi: 2, x_lo: 2; x = x_hi * 2 + x_lo), y: 4, z: 16, core: 2. Of those that a mesh axis runs over, the one named last changes fastest.
Arguments:
- images: bfloat16 [2560, 2, 48, 256], P('dp'), may hold values from -420 to 420
- references: bfloat16 [256, 2, 48, 256], P('cls'), may hold values from -0.12 to 0.12
- ctf_rows: float32 [64, 48], replicated, may hold values from 0.2 to 1
- group_ids: int32 [2560], P('dp'), may hold values from 0 to 63
- noise_var: float32 [48], replicated, may hold values from 0.5 to 2
- class_prior: float32 [256], P('cls'), may hold values from 0.5 to 2
Outputs:
- new_references: float32 [256, 24576], P('cls', 'dp')
- occupancy: float32 [256], P('cls')
- log_evidence: float32 [2560], P('dp')
The draws below stay inside these ranges and needn't reach their ends.
All inputs are finite; a program needn't handle non-finite values.
Results may differ from the reference program's by a relative error of at most 0.0071.
Values sent between devices are 32-bit elements; how exact they have to be, the bound alone decides.
A program may use at most 64 MiB of HBM per device.

```python
import math
import jax
import jax.numpy as jnp
from jax import lax

IMG_DEV = 80
CYCLES = 48
HARM = 256
ROT = 36
GROUPS = 64
IMAGES = 2560
CLASSES = 256
N_DP = 32


def shared_refs(key):
    refkey = jax.random.fold_in(key, 5)
    values = jnp.clip(jax.random.normal(refkey, (CLASSES, 2, CYCLES, HARM), jnp.float32), -6.0, 6.0)
    return values * 0.02


def draw_references(key, part):
    refs = shared_refs(key)
    return refs.astype(jnp.bfloat16)


def draw_images(key, part):
    refs = shared_refs(key)
    key = jax.random.fold_in(key, 11)
    first = jax.random.fold_in(key, 0)
    third = jax.random.fold_in(key, 2)
    fourth = jax.random.fold_in(key, 3)
    shape = (IMAGES, 2, CYCLES, HARM)
    values = jnp.clip(jax.random.normal(first, shape, jnp.float32), -4.0, 4.0)
    chosen = jax.random.randint(third, (IMAGES,), 0, CLASSES)
    strength = jnp.exp(jax.random.uniform(fourth, (IMAGES,), jnp.float32, math.log(150.0), math.log(500.0)))
    aligned = (jnp.arange(IMAGES, dtype=jnp.int32) % 4 == 0).astype(jnp.float32)
    amplitude = aligned * strength / (0.0008 * CYCLES * HARM)
    values = values + amplitude[:, None, None, None] * refs[chosen]
    return jnp.clip(values, -420.0, 420.0).astype(jnp.bfloat16)


def with_ends(values, stream_key, smallest, largest):
    place = [jax.random.randint(jax.random.fold_in(stream_key, axis), (), 0, length) for axis, length in enumerate(values.shape)]
    longest = values.shape.index(max(values.shape))
    next_to = place[:longest] + [(place[longest] + 1) % values.shape[longest]] + place[longest + 1:]
    return values.at[tuple(place)].set(smallest).at[tuple(next_to)].set(largest)


def steps_of(key, shape, shards, smallest, largest):
    factor_of = 1.0
    for dim, blocks in shards:
        draws = jax.random.uniform(jax.random.fold_in(jax.random.fold_in(key, 6), dim), (blocks,), jnp.float32, smallest / len(shards), largest / len(shards))
        factor_of = factor_of * jnp.repeat(jnp.exp(draws), shape[dim] // blocks).reshape((-1,) + (1,) * (len(shape) - 1 - dim))
    return factor_of


def setup_inputs(seed: int = 0) -> dict:
    key_of = jax.random.split(jax.random.key(seed), 7)
    images = draw_images(jax.random.fold_in(key_of[6], 71), 0)
    references = draw_references(jax.random.fold_in(key_of[6], 71), 0)
    ctf_rows = jnp.clip(jax.random.uniform(key_of[2], (GROUPS, CYCLES), jnp.float32, 0.2, 1.0), 0.2, 1.0)
    group_ids = with_ends(jax.random.randint(key_of[3], (IMAGES,), 0, GROUPS), jax.random.fold_in(key_of[3], 1), 0, GROUPS - 1).astype(jnp.int32)
    noise_var = jnp.clip(jnp.exp(jax.random.uniform(key_of[4], (CYCLES,), jnp.float32, math.log(0.5), math.log(2.0))), 0.5, 2.0)
    class_prior = jnp.clip(jnp.exp(math.log(2.0) - 1.3862944 * jax.random.uniform(key_of[5], (CLASSES,), jnp.float32) ** steps_of(key_of[5], (CLASSES,), ((0, 16),), -0.2, 0.2)), 0.5, 2.0)
    return dict(images=images, references=references, ctf_rows=ctf_rows, group_ids=group_ids, noise_var=noise_var, class_prior=class_prior)


def rotation_table(harmonics, rotations):
    product = (jnp.arange(harmonics, dtype=jnp.int32)[:, None] * jnp.arange(rotations, dtype=jnp.int32)[None, :]) % rotations
    angle = product.astype(jnp.float32) * (2.0 * math.pi / rotations)
    return jnp.concatenate([jnp.cos(angle), jnp.sin(angle)], axis=0)


def reference(images, references, ctf_rows, group_ids, noise_var, class_prior):
    hp = lax.Precision.HIGHEST
    table = rotation_table(HARM, ROT)
    refs32 = references.astype(jnp.float32)
    swapped = jnp.stack([refs32[:, 1], -refs32[:, 0]], axis=1)
    stacked = jnp.stack([refs32, swapped], axis=1)
    cycle_power = jnp.sum(refs32 * refs32, axis=(1, 3))
    log_prior = jnp.log(class_prior)
    image_blocks = images.reshape(N_DP, IMG_DEV, 2, CYCLES, HARM)
    group_blocks = group_ids.reshape(N_DP, IMG_DEV)

    def one_block(carry, block):
        numer, denom, masses = carry
        block_images, block_groups = block
        ctf = ctf_rows[block_groups]
        weight = ctf / noise_var[None, :]
        power_weight = ctf * ctf / noise_var[None, :]
        weighted = (block_images.astype(jnp.float32) * weight[:, None, :, None]).astype(jnp.bfloat16)
        weighted32 = weighted.astype(jnp.float32)
        cross = jnp.einsum('iprm,cqprm->icqm', weighted32, stacked)
        correlation = jnp.dot(cross.reshape(-1, 2 * HARM), table, precision=hp).reshape(IMG_DEV, CLASSES, ROT)
        model_power = jnp.dot(power_weight, cycle_power.T, precision=hp)
        score = correlation - 0.5 * model_power[:, :, None] + log_prior[None, :, None]
        peak = jnp.max(score, axis=(1, 2))
        total = jnp.sum(jnp.exp(score - peak[:, None, None]), axis=(1, 2))
        evidence = peak + jnp.log(total)
        posterior = jnp.exp(score - evidence[:, None, None])
        back = jnp.dot(posterior.reshape(-1, ROT), table.T, precision=hp).reshape(IMG_DEV, CLASSES, 2, HARM)
        back = back.astype(jnp.bfloat16).astype(jnp.float32)
        back_stack = jnp.stack([jnp.stack([back[:, :, 0], -back[:, :, 1]], axis=2), jnp.stack([back[:, :, 1], back[:, :, 0]], axis=2)], axis=2)
        numer = numer + jnp.einsum('icopm,iprm->corm', back_stack, weighted32)
        mass = jnp.sum(posterior, axis=2)
        denom = denom + jnp.dot(mass.T, power_weight, precision=hp)
        masses = masses + jnp.sum(mass, axis=0)
        return (numer, denom, masses), evidence

    init = (jnp.zeros((CLASSES, 2, CYCLES, HARM), jnp.float32), jnp.zeros((CLASSES, CYCLES), jnp.float32), jnp.zeros((CLASSES,), jnp.float32))
    (numer, denom, masses), evidence = lax.scan(one_block, init, (image_blocks, group_blocks))
    new_references = (numer / (denom[:, None, :, None] + 1.0)).reshape(CLASSES, 2 * CYCLES * HARM)
    occupancy = masses * (CLASSES / IMAGES)
    return new_references, occupancy, evidence.reshape(IMAGES)
```

```python
import functools
import math

import jax
import jax.numpy as jnp
from jax import lax
from jax.experimental import pallas as pl
from jax.experimental.pallas import tpu as pltpu
from jax.sharding import PartitionSpec as P

ROT = 36
HALF = ROT // 2
LANES = 128
SIDE = 64
HP = lax.Precision.HIGHEST
F32 = jnp.float32
BF16 = jnp.bfloat16
NT = (((1,), (1,)), ((), ()))
TN = (((0,), (0,)), ((), ()))
MESH = pl.DeviceIdType.MESH


def iota(shape, dim):
    return lax.broadcasted_iota(jnp.int32, shape, dim)


def half_transform(even, odd):
    quarter = HALF // 2
    even_sum = [even[b] + even[HALF - b] for b in range(quarter)]
    even_diff = [even[b] - even[HALF - b] for b in range(quarter)]
    odd_sum = [None] + [odd[b] + odd[HALF - b] for b in range(1, quarter)]
    odd_diff = [None] + [odd[b] - odd[HALF - b] for b in range(1, quarter)]
    cosines, sines = [], []
    for k in range(HALF + 1):
        source = even_sum if k % 2 == 0 else even_diff
        total = source[0]
        for b in range(1, quarter):
            total = total + source[b] * math.cos(math.pi * ((b * k) % ROT) / HALF)
        if k % 2 == 0:
            total = total + even[quarter] * (1.0 if k % 4 == 0 else -1.0)
        cosines.append(total)
    for k in range(HALF + 1):
        if k in (0, HALF):
            sines.append(None)
            continue
        source = odd_sum if k % 2 == 1 else odd_diff
        total = source[1] * math.sin(math.pi * k / HALF)
        for b in range(2, quarter):
            total = total + source[b] * math.sin(math.pi * ((b * k) % ROT) / HALF)
        if k % 2 == 1:
            total = total + odd[quarter] * (1.0 if k % 4 == 1 else -1.0)
        sines.append(total)
    return cosines, sines


def folds(harmonics):
    return -(-harmonics // ROT)


def score_kernel(
    image_ref, refs_ref, ids_ref, ctf_ref, noise_ref, prior_ref,
    w_ref, score_ref, stats_ref, power_ref,
    x_ref, xr_ref, s_ref,
):
    images, _, cycles, harm = image_ref.shape
    classes = refs_ref.shape[0]
    groups = ctf_ref.shape[0]
    count = folds(harm)
    rows = count * ROT
    onehot = (iota((groups, images), 0) == ids_ref[...]).astype(F32)
    ctf = lax.dot_general(onehot, ctf_ref[...], TN, precision=HP, preferred_element_type=F32)
    power = ctf * ctf / noise_ref[...]
    spread = (iota((cycles, LANES), 1) % SIDE == iota((cycles, LANES), 0)).astype(F32)
    weight = jnp.dot(ctf / noise_ref[...], spread, precision=HP, preferred_element_type=F32)
    power_lanes = jnp.dot(power, spread, precision=HP, preferred_element_type=F32)
    share = power_ref.shape[0] // 8
    share = cycles // share
    row = iota((power_ref.shape[0], cycles), 0)
    pick = ((row // 8) * share + row % 8 == iota((power_ref.shape[0], cycles), 1)) & (row % 8 < share)
    by_dest = lax.dot_general(pick.astype(F32), power, NT, precision=HP, preferred_element_type=F32)
    power_ref[...] = by_dest + (iota(by_dest.shape, 0) % 8 == share).astype(F32)

    eye = (iota((harm, harm), 0) == iota((harm, harm), 1)).astype(BF16)
    gap = jnp.zeros((SIDE - cycles, harm), BF16)

    def move(first, second, out_ref, at0, at1):
        block = jnp.concatenate([first[0], gap, first[1], gap, second[0], gap, second[1], gap], axis=0)
        turned = lax.dot_general(eye, block, NT, preferred_element_type=F32)
        out_ref[pl.ds(at0 * rows, harm), :] = turned[:, :LANES]
        out_ref[pl.ds(at1 * rows, harm), :] = turned[:, LANES:]
        if rows > harm:
            out_ref[pl.ds(at0 * rows + harm, rows - harm), :] = jnp.zeros((rows - harm, LANES), F32)
            out_ref[pl.ds(at1 * rows + harm, rows - harm), :] = jnp.zeros((rows - harm, LANES), F32)

    @pl.loop(0, images // 2)
    def _(pair):
        i = pair * 2
        move(
            (image_ref[i, 0], image_ref[i, 1]), (image_ref[i + 1, 0], image_ref[i + 1, 1]), x_ref, i, i + 1
        )

    @pl.loop(0, classes)
    def _(c):
        real, imag = refs_ref[c, 0], refs_ref[c, 1]
        move((real, imag), (imag, -real), xr_ref, c, classes + c)

    def one_residue(b, squares):
        image_parts, ref_parts = [], []
        for a in range(count):
            at = b + ROT * a
            x = x_ref[pl.ds(at, images, stride=rows), :] * weight
            r = xr_ref[pl.ds(at, 2 * classes, stride=rows), :]
            squares = squares + r[:classes] * r[:classes]
            x, r = x.astype(BF16), r.astype(BF16)
            w_ref[b, :, a * LANES : (a + 1) * LANES] = x
            image_parts.append(x)
            ref_parts.append(r)
        s_ref[b] = lax.dot_general(
            jnp.concatenate(ref_parts, axis=1),
            jnp.concatenate(image_parts, axis=1),
            NT,
            preferred_element_type=F32,
        )
        return squares

    squares = lax.fori_loop(0, ROT, one_residue, jnp.zeros((classes, LANES), F32))
    model = lax.dot_general(squares, power_lanes, NT, precision=HP, preferred_element_type=F32)
    log_prior = jnp.sum(
        jnp.where(iota((classes, classes), 0) == iota((classes, classes), 1), jnp.log(prior_ref[...]), 0.0),
        axis=1,
        keepdims=True,
    )
    base = log_prior - 0.5 * model
    real = [s_ref[b, :classes] for b in range(ROT)]
    imag = [s_ref[b, classes:] for b in range(ROT)]
    even = [real[0]] + [real[b] + real[ROT - b] for b in range(1, HALF)] + [real[HALF]]
    odd = [None] + [imag[b] - imag[ROT - b] for b in range(1, HALF)]
    cosines, sines = half_transform(even, odd)
    peak = None
    for k in range(HALF + 1):
        if sines[k] is None:
            made = [(k, cosines[k] + base)]
        else:
            centre = cosines[k] + base
            made = [(k, centre + sines[k]), (ROT - k, centre - sines[k])]
        for at, value in made:
            score_ref[at] = value
            peak = value if peak is None else jnp.maximum(peak, value)
    peak = jnp.max(peak, axis=0, keepdims=True)
    total = jnp.zeros((classes, images), F32)
    for k in range(ROT):
        total = total + jnp.exp(score_ref[k] - peak)
    total = jnp.sum(total, axis=0, keepdims=True)
    stats_ref[...] = jnp.zeros(stats_ref.shape, F32)
    stats_ref[0:1, 0:images] = peak
    stats_ref[1:2, 0:images] = total


def update_kernel(
    scale, w_ref, score_ref, stats_ref, power_ref,
    out_ref, occ_ref, evidence_ref,
    gath_ref, back_ref, y_ref, t_ref, l_ref, r_ref, last_ref,
    gath_send, gath_recv, ring_send, ring_recv, last_send, last_recv,
):
    classes, images = score_ref.shape[1:]
    halves = t_ref.shape[0]
    harm = halves * LANES
    count = w_ref.shape[2] // LANES
    rows = count * ROT
    depth = l_ref.shape[0]
    share = out_ref.shape[1] // harm
    blocks = out_ref.shape[1] // LANES
    dp, cls = lax.axis_index("dp"), lax.axis_index("cls")
    n_cls = lax.axis_size("cls")
    x, z = dp // depth, dp % depth

    def at_z(step):
        return (z + step + depth) % depth

    up, down = x * depth + at_z(1), x * depth + at_z(-1)
    across = (1 - x) * depth + z
    barrier = pltpu.get_barrier_semaphore()
    for j in range(1, n_cls):
        pl.semaphore_signal(barrier, inc=1, device_id={"dp": dp, "cls": (cls + j) % n_cls}, device_id_type=MESH)
    for other in (up, down, across):
        pl.semaphore_signal(barrier, inc=1, device_id={"dp": other, "cls": cls}, device_id_type=MESH)
    pl.semaphore_wait(barrier, n_cls - 1 + 3)

    sends = []
    for j in range(1, n_cls):
        copy = pltpu.make_async_remote_copy(
            src_ref=stats_ref,
            dst_ref=gath_ref.at[j],
            send_sem=gath_send.at[j],
            recv_sem=gath_recv.at[j],
            device_id={"dp": dp, "cls": (cls + j) % n_cls},
            device_id_type=MESH,
        )
        copy.start()
        sends.append(copy)
    for copy in sends:
        copy.wait_recv()
    parts = [stats_ref[...]] + [gath_ref[j] for j in range(1, n_cls)]
    peak = parts[0][0:1, :images]
    for part in parts[1:]:
        peak = jnp.maximum(peak, part[0:1, :images])
    total = jnp.zeros((1, images), F32)
    for part in parts:
        total = total + part[1:2, :images] * jnp.exp(part[0:1, :images] - peak)
    evidence = peak + jnp.log(total)
    evidence_ref[...] = evidence

    posterior = [jnp.exp(score_ref[k] - evidence) for k in range(ROT)]
    even = [posterior[0]] + [posterior[k] + posterior[ROT - k] for k in range(1, HALF)] + [posterior[HALF]]
    odd = [None] + [posterior[k] - posterior[ROT - k] for k in range(1, HALF)]
    cosines, sines = half_transform(even, odd)
    mass = cosines[0]
    for b in range(HALF + 1):
        real = cosines[b].astype(BF16)
        imag = jnp.zeros((classes, images), BF16) if sines[b] is None else sines[b].astype(BF16)
        back_ref[b] = jnp.concatenate([real, imag], axis=0)
        if 0 < b < HALF:
            back_ref[ROT - b] = jnp.concatenate([real, -imag], axis=0)
    denominators = lax.dot_general(power_ref[...], mass, NT, precision=HP, preferred_element_type=F32)

    sign = jnp.where(iota((classes, LANES), 1) < SIDE, -1.0, 1.0)

    @pl.loop(0, ROT)
    def _(b):
        both = jnp.dot(back_ref[b], w_ref[b], preferred_element_type=F32)
        for a in range(count):
            piece = both[:, a * LANES : (a + 1) * LANES]
            y_ref[pl.ds(b + ROT * a, classes, stride=rows), :] = piece[:classes] + sign * pltpu.roll(
                piece[classes:], SIDE, 1
            )

    @pl.loop(0, classes)
    def _(c):
        for h in range(halves):
            t_ref[h, pl.ds(pl.multiple_of(c * LANES, LANES), LANES), :] = y_ref[
                pl.ds(pl.multiple_of(c * rows + h * LANES, 8), LANES), :
            ].T

    for dest in range(depth):
        for p in range(2):
            for j in range(share):
                row = p * SIDE + dest * share + j
                for h in range(halves):
                    l_ref[dest, p, (j * halves + h) * classes : (j * halves + h + 1) * classes, :] = t_ref[
                        h, pl.ds(row, classes, stride=LANES), :
                    ]
            tail = l_ref.shape[2] - 8
            l_ref[dest, p, tail:, :] = jnp.zeros((8, LANES), F32)
            l_ref[dest, p, tail:, 0:classes] = denominators[dest * 8 : dest * 8 + 8]

    hops = depth // 2
    streams = [(1, 0, hops), (-1, 1, hops), (1, 1, hops - 1), (-1, 0, hops - 1)]

    def hop(index, t, source):
        step, p, _ = streams[index]
        return pltpu.make_async_remote_copy(
            src_ref=source,
            dst_ref=r_ref.at[index, t],
            send_sem=ring_send.at[index, t],
            recv_sem=ring_recv.at[index, t],
            device_id={"dp": up if step == 1 else down, "cls": cls},
            device_id_type=MESH,
        )

    for index, (step, p, length) in enumerate(streams):
        hop(index, 0, l_ref.at[at_z(step * length), p]).start()

    def one_hop(t, carry):
        for index, (step, p, length) in enumerate(streams):

            def go():
                hop(index, t - 1, l_ref.at[0, p]).wait_recv()
                r_ref[index, t - 1] = r_ref[index, t - 1] + l_ref[at_z(step * (length - t)), p]
                hop(index, t, r_ref.at[index, t - 1]).start()

            if length == hops:
                go()
            else:
                pl.when(t < length)(go)
        return carry

    lax.fori_loop(1, hops, one_hop, 0)
    for index, (step, p, length) in enumerate(streams):
        hop(index, length - 1, l_ref.at[0, p]).wait_recv()
    ends = [streams[index][2] - 1 for index in range(4)]
    sums = [
        l_ref[z, 0] + r_ref[0, ends[0]] + r_ref[3, ends[3]],
        l_ref[z, 1] + r_ref[1, ends[1]] + r_ref[2, ends[2]],
    ]
    last_ref[0] = jnp.where(x == 0, sums[1], sums[0])
    copy = pltpu.make_async_remote_copy(
        src_ref=last_ref.at[0],
        dst_ref=last_ref.at[1],
        send_sem=last_send,
        recv_sem=last_recv,
        device_id={"dp": across, "cls": cls},
        device_id_type=MESH,
    )
    copy.start()
    mine = jnp.where(x == 0, sums[0], sums[1])
    copy.wait_recv()
    mine = mine + last_ref[1]
    tail = mine[blocks * classes :, :]
    occ_ref[...] = tail[share : share + 1, 0:classes] * scale
    columns = jnp.concatenate([tail, jnp.zeros((LANES - 8, LANES), F32)], axis=0).T
    for j in range(share):
        below = columns[:classes, j : j + 1] + 1.0
        for h in range(halves):
            q = j * halves + h
            out_ref[:, q * LANES : (q + 1) * LANES] = mine[q * classes : (q + 1) * classes] / below
    copy.wait_send()
    for send in sends:
        send.wait_send()
    for index, (step, p, length) in enumerate(streams):

        def drained(t, carry):
            hop(index, t, l_ref.at[0, p]).wait_send()
            return carry

        lax.fori_loop(0, length, drained, 0)


def vmem(count):
    return [pl.BlockSpec(memory_space=pltpu.VMEM)] * count


def shards(images, references, ctf_rows, group_ids, noise_var, class_prior):
    img_count, _, cycles, harm = images.shape
    classes = references.shape[0]
    n_dp, n_cls = lax.axis_size("dp"), lax.axis_size("cls")
    depth = n_dp // 2
    share = cycles // depth
    count = folds(harm)
    rows = count * ROT
    width = share * harm
    w, score, stats, power = pl.pallas_call(
        score_kernel,
        out_shape=[
            jax.ShapeDtypeStruct((ROT, img_count, count * LANES), BF16),
            jax.ShapeDtypeStruct((ROT, classes, img_count), F32),
            jax.ShapeDtypeStruct((8, LANES), F32),
            jax.ShapeDtypeStruct((depth * 8, img_count), F32),
        ],
        in_specs=vmem(6),
        out_specs=vmem(4),
        scratch_shapes=[
            pltpu.VMEM((img_count * rows, LANES), F32),
            pltpu.VMEM((2 * classes * rows, LANES), F32),
            pltpu.VMEM((ROT, 2 * classes, img_count), F32),
        ],
        compiler_params=pltpu.CompilerParams(vmem_limit_bytes=48 * 2**20),
    )(
        images, references, group_ids.reshape(1, -1), ctf_rows, noise_var.reshape(1, -1),
        class_prior.reshape(1, -1),
    )
    chunk = width // LANES * classes + 8
    new_references, occupancy, evidence = pl.pallas_call(
        functools.partial(update_kernel, classes * n_cls / (img_count * n_dp)),
        out_shape=[
            jax.ShapeDtypeStruct((classes, width), F32),
            jax.ShapeDtypeStruct((1, classes), F32),
            jax.ShapeDtypeStruct((1, img_count), F32),
        ],
        in_specs=vmem(4),
        out_specs=vmem(3),
        scratch_shapes=[
            pltpu.VMEM((n_cls, 8, LANES), F32),
            pltpu.VMEM((ROT, 2 * classes, img_count), BF16),
            pltpu.VMEM((classes * rows, LANES), F32),
            pltpu.VMEM((harm // LANES, classes * LANES, LANES), F32),
            pltpu.VMEM((depth, 2, chunk, LANES), F32),
            pltpu.VMEM((4, depth // 2, chunk, LANES), F32),
            pltpu.VMEM((2, chunk, LANES), F32),
            pltpu.SemaphoreType.DMA((n_cls,)),
            pltpu.SemaphoreType.DMA((n_cls,)),
            pltpu.SemaphoreType.DMA((4, depth // 2)),
            pltpu.SemaphoreType.DMA((4, depth // 2)),
            pltpu.SemaphoreType.DMA,
            pltpu.SemaphoreType.DMA,
        ],
        compiler_params=pltpu.CompilerParams(
            collective_id=0, has_side_effects=True, vmem_limit_bytes=48 * 2**20
        ),
    )(w, score, stats, power)
    return new_references, occupancy.reshape(-1), evidence.reshape(-1)


def solution(mesh):
    placed = (P("dp", None, None, None), P("cls", None, None, None), P(), P("dp"), P(), P("cls"))
    return jax.shard_map(
        shards,
        mesh=mesh,
        in_specs=placed,
        out_specs=(P("cls", "dp"), P("cls"), P("dp")),
        check_vma=False,
    )
```

```python
import functools
import math

import jax
import jax.numpy as jnp
from jax import lax
from jax.experimental import pallas as pl
from jax.experimental.pallas import tpu as pltpu
from jax.sharding import PartitionSpec as P

ROT = 36
HALF = ROT // 2
LANES = 128
SIDE = 64
HP = lax.Precision.HIGHEST
F32 = jnp.float32
BF16 = jnp.bfloat16
NT = (((1,), (1,)), ((), ()))
TN = (((0,), (0,)), ((), ()))
MESH = pl.DeviceIdType.MESH


def iota(shape, dim):
    return lax.broadcasted_iota(jnp.int32, shape, dim)


def half_transform(even, odd):
    quarter = HALF // 2
    even_sum = [even[b] + even[HALF - b] for b in range(quarter)]
    even_diff = [even[b] - even[HALF - b] for b in range(quarter)]
    odd_sum = [None] + [odd[b] + odd[HALF - b] for b in range(1, quarter)]
    odd_diff = [None] + [odd[b] - odd[HALF - b] for b in range(1, quarter)]
    cosines, sines = [], []
    for k in range(HALF + 1):
        source = even_sum if k % 2 == 0 else even_diff
        total = source[0]
        for b in range(1, quarter):
            total = total + source[b] * math.cos(math.pi * ((b * k) % ROT) / HALF)
        if k % 2 == 0:
            total = total + even[quarter] * (1.0 if k % 4 == 0 else -1.0)
        cosines.append(total)
    for k in range(HALF + 1):
        if k in (0, HALF):
            sines.append(None)
            continue
        source = odd_sum if k % 2 == 1 else odd_diff
        total = source[1] * math.sin(math.pi * k / HALF)
        for b in range(2, quarter):
            total = total + source[b] * math.sin(math.pi * ((b * k) % ROT) / HALF)
        if k % 2 == 1:
            total = total + odd[quarter] * (1.0 if k % 4 == 1 else -1.0)
        sines.append(total)
    return cosines, sines


def folds(harmonics):
    return -(-harmonics // ROT)


def column(row):
    square = (row.shape[1], row.shape[1])
    return jnp.sum(jnp.where(iota(square, 0) == iota(square, 1), row, 0.0), axis=1, keepdims=True)


def reduction_tree():
    parent = {}
    for sign in (1, -1):
        for ox in (0, 1):
            for leaf, relay in ((7, 6), (5, 6), (4, 3), (2, 3)):
                parent[(ox, leaf * sign)] = (ox, relay * sign)
        for relay in (6, 3, 1):
            parent[(1, relay * sign)] = (0, relay * sign)
            parent[(0, relay * sign)] = (0, 0)
    parent[(0, 8)] = (0, 6)
    parent[(1, 8)] = (1, -6)
    parent[(1, 0)] = (0, 0)
    return parent


ORDER = (8, 7, -7, 5, -5, 4, -4, 2, -2, 6, -6, 3, -3, 1, -1, 0)
PIECES = 5
STRIDE = 289


def kernel(
    scale, image_hbm, refs_hbm, ids_hbm, ctf_hbm, noise_hbm, prior_hbm,
    out_ref, occ_ref, evidence_ref,
    image_ref, refs_ref, ids_ref, ctf_ref, noise_ref, prior_ref,
    x_ref, xr_ref, w_ref, s_ref, score_ref, stats_ref, gath_ref, back_ref, y_ref, t_ref, den_ref, l_ref, r_ref,
    load_sem, gath_send, gath_recv, tree_send, tree_recv,
):
    images, _, cycles, harm = image_ref.shape
    classes = refs_ref.shape[0]
    groups = ctf_ref.shape[1]
    count = folds(harm)
    rows = count * ROT
    depth = l_ref.shape[0]
    share = cycles // depth
    halves = harm // LANES
    blocks = share * halves
    piece = images // PIECES

    dp, cls = lax.axis_index("dp"), lax.axis_index("cls")
    n_cls = lax.axis_size("cls")
    x, z = dp // depth, dp % depth

    def at_z(step):
        return (z + step + depth) % depth

    def at_x(step):
        return (x + step) % 2

    loads = [
        pltpu.make_async_copy(source, target, load_sem.at[n])
        for n, (source, target) in enumerate(
            [(ids_hbm, ids_ref), (ctf_hbm, ctf_ref), (noise_hbm, noise_ref), (prior_hbm, prior_ref), (refs_hbm, refs_ref)]
            + [(image_hbm.at[pl.ds(n * piece, piece)], image_ref.at[pl.ds(n * piece, piece)]) for n in range(PIECES)]
        )
    ]
    for load in loads:
        load.start()

    parent = reduction_tree()
    index = {node: n for n, node in enumerate(parent)}
    children = {node: [other for other in parent if parent[other] == node] for node in [*parent, (0, 0)]}
    moves = {((parent[node][0] - node[0]) % 2, (parent[node][1] - node[1]) % depth) for node in parent}
    peers = sorted(moves | {(ox, -oz % depth) for ox, oz in moves})
    barrier = pltpu.get_barrier_semaphore()
    for ox, oz in peers:
        pl.semaphore_signal(
            barrier, inc=1, device_id={"dp": at_x(ox) * depth + at_z(oz), "cls": cls}, device_id_type=MESH
        )
    for j in range(1, n_cls):
        pl.semaphore_signal(barrier, inc=1, device_id={"dp": dp, "cls": (cls + j) % n_cls}, device_id_type=MESH)

    def clear(ref, total, unroll):
        @pl.loop(0, total, unroll=unroll)
        def _(i):
            ref[pl.ds(i * STRIDE + harm, rows - harm), :] = jnp.zeros((rows - harm, LANES), F32)

    clear(x_ref, images, 8)
    clear(xr_ref, 2 * classes, 8)

    for load in loads[:4]:
        load.wait()
    onehot = (iota((groups, images), 0) == ids_ref[...]).astype(F32)
    ctf = jnp.dot(ctf_ref[...], onehot, precision=HP, preferred_element_type=F32)
    noise = column(noise_ref[...])
    power = ctf * ctf / noise
    spread = (iota((cycles, LANES), 1) % SIDE == iota((cycles, LANES), 0)).astype(F32)
    weight = lax.dot_general(ctf / noise, spread, TN, precision=HP, preferred_element_type=F32)
    power_lanes = lax.dot_general(power, spread, TN, precision=HP, preferred_element_type=F32)
    shape = (depth * 8, cycles)
    row = iota(shape, 0)
    pick = ((row // 8) * share + row % 8 == iota(shape, 1)) & (row % 8 < share)
    by_dest = jnp.dot(pick.astype(F32), power, precision=HP, preferred_element_type=F32)
    by_dest = by_dest + (iota(by_dest.shape, 0) % 8 == share).astype(F32)
    log_prior = column(jnp.log(prior_ref[...]))

    eye = (iota((harm, harm), 0) == iota((harm, harm), 1)).astype(BF16)
    gap = jnp.zeros((SIDE - cycles, harm), BF16)

    def turn(first, second, ref, at0, at1):
        block = jnp.concatenate([first[0], gap, first[1], gap, second[0], gap, second[1], gap], axis=0)
        turned = lax.dot_general(eye, block, NT, preferred_element_type=F32)
        ref[pl.ds(at0 * STRIDE, harm), :] = turned[:, :LANES]
        ref[pl.ds(at1 * STRIDE, harm), :] = turned[:, LANES:]

    loads[4].wait()

    @pl.loop(0, classes, unroll=8)
    def _(c):
        real, imag = refs_ref[c, 0], refs_ref[c, 1]
        turn((real, imag), (imag, -real), xr_ref, c, classes + c)

    for n in range(PIECES):
        loads[5 + n].wait()

        @pl.loop(0, piece // 2, unroll=8)
        def _(pair):
            i = n * piece + pair * 2
            turn((image_ref[i, 0], image_ref[i, 1]), (image_ref[i + 1, 0], image_ref[i + 1, 1]), x_ref, i, i + 1)

    def one_residue(b, squares):
        image_parts, ref_parts = [], []
        for a in range(count):
            at = b + ROT * a
            x_part = (x_ref[pl.ds(at, images, stride=STRIDE), :] * weight).astype(BF16)
            r_part = xr_ref[pl.ds(at, 2 * classes, stride=STRIDE), :]
            squares = squares + r_part[:classes] * r_part[:classes]
            w_ref[b, :, a * LANES : (a + 1) * LANES] = x_part
            image_parts.append(x_part)
            ref_parts.append(r_part.astype(BF16))
        s_ref[b] = lax.dot_general(
            jnp.concatenate(ref_parts, axis=1),
            jnp.concatenate(image_parts, axis=1),
            NT,
            preferred_element_type=F32,
        )
        return squares

    squares = lax.fori_loop(0, ROT, one_residue, jnp.zeros((classes, LANES), F32), unroll=12)
    model = lax.dot_general(squares, power_lanes, NT, precision=HP, preferred_element_type=F32)
    base = log_prior - 0.5 * model
    real = [s_ref[b, :classes] for b in range(ROT)]
    imag = [s_ref[b, classes:] for b in range(ROT)]
    even = [real[0]] + [real[b] + real[ROT - b] for b in range(1, HALF)] + [real[HALF]]
    odd = [None] + [imag[b] - imag[ROT - b] for b in range(1, HALF)]
    cosines, sines = half_transform(even, odd)
    peak = None
    for k in range(HALF + 1):
        centre = cosines[k] + base
        made = [(k, centre)] if sines[k] is None else [(k, centre + sines[k]), (ROT - k, centre - sines[k])]
        for at, value in made:
            score_ref[at] = value
            peak = value if peak is None else jnp.maximum(peak, value)
    peak = jnp.max(peak, axis=0, keepdims=True)
    total = jnp.zeros((classes, images), F32)
    for k in range(ROT):
        total = total + jnp.exp(score_ref[k] - peak)
    stats_ref[...] = jnp.zeros(stats_ref.shape, F32)
    stats_ref[0:1, 0:images] = peak
    stats_ref[1:2, 0:images] = jnp.sum(total, axis=0, keepdims=True)

    pl.semaphore_wait(barrier, len(peers) + n_cls - 1)
    sends = []
    for j in range(1, n_cls):
        copy = pltpu.make_async_remote_copy(
            src_ref=stats_ref,
            dst_ref=gath_ref.at[j],
            send_sem=gath_send.at[j],
            recv_sem=gath_recv.at[j],
            device_id={"dp": dp, "cls": (cls + j) % n_cls},
            device_id_type=MESH,
        )
        copy.start()
        sends.append(copy)
    for copy in sends:
        copy.wait_recv()
    parts = [stats_ref[...]] + [gath_ref[j] for j in range(1, n_cls)]
    peak = parts[0][0:1, :images]
    for part in parts[1:]:
        peak = jnp.maximum(peak, part[0:1, :images])
    total = jnp.zeros((1, images), F32)
    for part in parts:
        total = total + part[1:2, :images] * jnp.exp(part[0:1, :images] - peak)
    evidence = peak + jnp.log(total)
    evidence_ref[...] = evidence

    posterior = [jnp.exp(score_ref[k] - evidence) for k in range(ROT)]
    even = [posterior[0]] + [posterior[k] + posterior[ROT - k] for k in range(1, HALF)] + [posterior[HALF]]
    odd = [None] + [posterior[k] - posterior[ROT - k] for k in range(1, HALF)]
    cosines, sines = half_transform(even, odd)
    mass = cosines[0]
    for b in range(HALF + 1):
        real = cosines[b].astype(BF16)
        imag = jnp.zeros((classes, images), BF16) if sines[b] is None else sines[b].astype(BF16)
        back_ref[b] = jnp.concatenate([real, imag], axis=0)
        if 0 < b < HALF:
            back_ref[ROT - b] = jnp.concatenate([real, -imag], axis=0)
    den_ref[...] = jnp.zeros(den_ref.shape, F32)
    den_ref[:, 0:classes] = lax.dot_general(by_dest, mass, NT, precision=HP, preferred_element_type=F32)

    sign = jnp.where(iota((classes, LANES), 1) < SIDE, -1.0, 1.0)

    @pl.loop(0, ROT, unroll=12)
    def _(b):
        both = jnp.dot(back_ref[b], w_ref[b], preferred_element_type=F32)
        for a in range(count):
            part = both[:, a * LANES : (a + 1) * LANES]
            y_ref[pl.ds(b + ROT * a, classes, stride=STRIDE), :] = part[:classes] + sign * pltpu.roll(
                part[classes:], SIDE, 1
            )

    @pl.loop(0, classes, unroll=4)
    def _(c):
        for h in range(halves):
            t_ref[h, pl.ds(pl.multiple_of(c * LANES, LANES), LANES), :] = y_ref[
                pl.ds(c * STRIDE + h * LANES, LANES), :
            ].T

    def towards(node, source):
        ox, oz = parent[node][0] - node[0], parent[node][1] - node[1]
        return pltpu.make_async_remote_copy(
            src_ref=source,
            dst_ref=r_ref.at[index[node]],
            send_sem=tree_send.at[index[node]],
            recv_sem=tree_recv.at[index[node]],
            device_id={"dp": at_x(ox % 2) * depth + at_z(oz % depth), "cls": cls},
            device_id_type=MESH,
        )

    def send(node):
        towards(node, l_ref.at[at_z(-node[1]), at_x(node[0])]).start()

    def gathered(node):
        value = l_ref[at_z(-node[1]), at_x(node[0])]
        for child in children[node]:
            towards(child, l_ref.at[0, 0]).wait_recv()
            value = value + r_ref[index[child]]
        return value

    def pass_on(node):
        l_ref[at_z(-node[1]), at_x(node[0])] = gathered(node)
        send(node)

    for oz in ORDER:
        dest = at_z(-oz)
        for p in range(2):
            for j in range(share):
                first = p * SIDE + dest * share + j
                for h in range(halves):
                    q = j * halves + h
                    l_ref[dest, p, q * classes : (q + 1) * classes, :] = t_ref[
                        h, pl.ds(first, classes, stride=LANES), :
                    ]
            l_ref[dest, p, blocks * classes :, :] = den_ref[pl.ds(pl.multiple_of(dest * 8, 8), 8), :]
        for ox in (0, 1):
            if (ox, oz) in parent and not children[(ox, oz)]:
                send((ox, oz))
    for node in ((1, 6), (1, -6), (1, 3), (1, -3), (0, 6), (0, -6), (0, 3), (0, -3), (0, 1), (0, -1)):
        pass_on(node)
    mine = gathered((0, 0))
    tail = mine[blocks * classes :, :]
    occ_ref[...] = tail[share : share + 1, 0:classes] * scale
    columns = jnp.concatenate([tail, jnp.zeros((LANES - 8, LANES), F32)], axis=0).T
    for j in range(share):
        below = columns[:classes, j : j + 1] + 1.0
        for h in range(halves):
            q = j * halves + h
            out_ref[:, q * LANES : (q + 1) * LANES] = mine[q * classes : (q + 1) * classes] / below
    for copy in sends:
        copy.wait_send()
    for node in parent:
        towards(node, l_ref.at[0, 0]).wait_send()


def shards(images, references, ctf_rows, group_ids, noise_var, class_prior):
    img_count, _, cycles, harm = images.shape
    classes = references.shape[0]
    n_dp, n_cls = lax.axis_size("dp"), lax.axis_size("cls")
    depth = n_dp // 2
    count = folds(harm)
    rows = count * ROT
    width = cycles // depth * harm
    chunk = width // LANES * classes + 8
    nodes = len(reduction_tree())
    args = (
        images, references, group_ids.reshape(1, -1), ctf_rows.T, noise_var.reshape(1, -1), class_prior.reshape(1, -1)
    )
    new_references, occupancy, evidence = pl.pallas_call(
        functools.partial(kernel, classes * n_cls / (img_count * n_dp)),
        out_shape=[
            jax.ShapeDtypeStruct((classes, width), F32),
            jax.ShapeDtypeStruct((1, classes), F32),
            jax.ShapeDtypeStruct((1, img_count), F32),
        ],
        in_specs=[pl.BlockSpec(memory_space=pl.ANY)] * len(args),
        out_specs=[pl.BlockSpec(memory_space=pltpu.VMEM)] * 3,
        scratch_shapes=[
            *[pltpu.VMEM(arg.shape, arg.dtype) for arg in args],
            pltpu.VMEM((img_count * STRIDE, LANES), F32),
            pltpu.VMEM((2 * classes * STRIDE, LANES), F32),
            pltpu.VMEM((ROT, img_count, count * LANES), BF16),
            pltpu.VMEM((ROT, 2 * classes, img_count), F32),
            pltpu.VMEM((ROT, classes, img_count), F32),
            pltpu.VMEM((8, LANES), F32),
            pltpu.VMEM((n_cls, 8, LANES), F32),
            pltpu.VMEM((ROT, 2 * classes, img_count), BF16),
            pltpu.VMEM((classes * STRIDE, LANES), F32),
            pltpu.VMEM((harm // LANES, classes * LANES, LANES), F32),
            pltpu.VMEM((depth * 8, LANES), F32),
            pltpu.VMEM((depth, 2, chunk, LANES), F32),
            pltpu.VMEM((nodes, chunk, LANES), F32),
            pltpu.SemaphoreType.DMA((5 + PIECES,)),
            pltpu.SemaphoreType.DMA((n_cls,)),
            pltpu.SemaphoreType.DMA((n_cls,)),
            pltpu.SemaphoreType.DMA((nodes,)),
            pltpu.SemaphoreType.DMA((nodes,)),
        ],
        compiler_params=pltpu.CompilerParams(
            collective_id=0, has_side_effects=True, vmem_limit_bytes=56 * 2**20
        ),
    )(*args)
    return new_references, occupancy.reshape(-1), evidence.reshape(-1)


def solution(mesh):
    placed = (P("dp", None, None, None), P("cls", None, None, None), P(), P("dp"), P(), P("cls"))
    return jax.shard_map(
        shards,
        mesh=mesh,
        in_specs=placed,
        out_specs=(P("cls", "dp"), P("cls"), P("dp")),
        check_vma=False,
    )
```

```python
import functools
import math

import jax
import jax.numpy as jnp
from jax import lax
from jax.experimental import pallas as pl
from jax.experimental.pallas import tpu as pltpu
from jax.sharding import PartitionSpec as P

ROT = 36
HALF = ROT // 2
LANES = 128
SIDE = 64
HP = lax.Precision.HIGHEST
F32 = jnp.float32
BF16 = jnp.bfloat16
NT = (((1,), (1,)), ((), ()))
TN = (((0,), (0,)), ((), ()))
MESH = pl.DeviceIdType.MESH


def iota(shape, dim):
    return lax.broadcasted_iota(jnp.int32, shape, dim)


def half_transform(even, odd):
    quarter = HALF // 2
    even_sum = [even[b] + even[HALF - b] for b in range(quarter)]
    even_diff = [even[b] - even[HALF - b] for b in range(quarter)]
    odd_sum = [None] + [odd[b] + odd[HALF - b] for b in range(1, quarter)]
    odd_diff = [None] + [odd[b] - odd[HALF - b] for b in range(1, quarter)]
    cosines, sines = [], []
    for k in range(HALF + 1):
        source = even_sum if k % 2 == 0 else even_diff
        total = source[0]
        for b in range(1, quarter):
            total = total + source[b] * math.cos(math.pi * ((b * k) % ROT) / HALF)
        if k % 2 == 0:
            total = total + even[quarter] * (1.0 if k % 4 == 0 else -1.0)
        cosines.append(total)
    for k in range(HALF + 1):
        if k in (0, HALF):
            sines.append(None)
            continue
        source = odd_sum if k % 2 == 1 else odd_diff
        total = source[1] * math.sin(math.pi * k / HALF)
        for b in range(2, quarter):
            total = total + source[b] * math.sin(math.pi * ((b * k) % ROT) / HALF)
        if k % 2 == 1:
            total = total + odd[quarter] * (1.0 if k % 4 == 1 else -1.0)
        sines.append(total)
    return cosines, sines


def folds(harmonics):
    return -(-harmonics // ROT)


def column(row):
    square = (row.shape[1], row.shape[1])
    return jnp.sum(jnp.where(iota(square, 0) == iota(square, 1), row, 0.0), axis=1, keepdims=True)


PARENT = {
    (1, 7): (0, 7), (0, 8): (0, 7), (1, 8): (1, -7), (1, 6): (1, 5), (1, 3): (0, 3), (1, -5): (0, -5),
    (1, -3): (1, -2), (0, -7): (0, -6), (0, 5): (0, 4), (0, 7): (0, 6), (1, -7): (0, -6), (1, -6): (0, -6),
    (1, 5): (1, 4), (1, -2): (0, -2), (0, 3): (0, 2), (0, -5): (0, -4), (0, 6): (0, 4), (0, -3): (0, -2),
    (1, 2): (0, 2), (1, 4): (0, 4), (0, -6): (0, -4), (1, -4): (0, -4), (0, 2): (0, 1), (1, 0): (0, 0),
    (1, -1): (0, -1), (0, -2): (0, -1), (1, 1): (0, 1), (0, 4): (0, 0), (0, -4): (0, 0), (0, 1): (0, 0),
    (0, -1): (0, 0),
}
PIECES = 5
STRIDE = 289


def kernel(
    scale, image_hbm, refs_hbm, small_hbm,
    out_ref, occ_ref, evidence_ref,
    image_ref, refs_ref, small_ref,
    x_ref, xr_ref, w_ref, s_ref, even_ref, odd_ref, stats_ref, gath_ref, back_ref, y_ref, t_ref, den_ref, l_ref, r_ref,
    load_sem, gath_send, gath_recv, tree_send, tree_recv,
):
    images, _, cycles, harm = image_ref.shape
    classes = refs_ref.shape[0]
    count = folds(harm)
    rows = count * ROT
    depth = l_ref.shape[0]
    share = cycles // depth
    halves = harm // LANES
    blocks = share * halves
    piece = images // PIECES

    dp, cls = lax.axis_index("dp"), lax.axis_index("cls")
    n_cls = lax.axis_size("cls")
    x, z = dp // depth, dp % depth

    def at_z(step):
        return (z + step + depth) % depth

    def at_x(step):
        return (x + step) % 2

    loads = [
        pltpu.make_async_copy(source, target, load_sem.at[n])
        for n, (source, target) in enumerate(
            [(small_hbm, small_ref), (refs_hbm, refs_ref)]
            + [(image_hbm.at[pl.ds(n * piece, piece)], image_ref.at[pl.ds(n * piece, piece)]) for n in range(PIECES)]
        )
    ]
    for load in loads:
        load.start()

    parent = PARENT
    index = {node: n for n, node in enumerate(parent)}
    children = {node: [other for other in parent if parent[other] == node] for node in [*parent, (0, 0)]}
    moves = {((parent[node][0] - node[0]) % 2, (parent[node][1] - node[1]) % depth) for node in parent}
    peers = sorted(moves | {(ox, -oz % depth) for ox, oz in moves})
    barrier = pltpu.get_barrier_semaphore()
    for ox, oz in peers:
        pl.semaphore_signal(
            barrier, inc=1, device_id={"dp": at_x(ox) * depth + at_z(oz), "cls": cls}, device_id_type=MESH
        )
    for j in range(1, n_cls):
        pl.semaphore_signal(barrier, inc=1, device_id={"dp": dp, "cls": (cls + j) % n_cls}, device_id_type=MESH)

    def clear(ref, total, unroll):
        @pl.loop(0, total, unroll=unroll)
        def _(i):
            ref[pl.ds(i * STRIDE + harm, rows - harm), :] = jnp.zeros((rows - harm, LANES), F32)

    clear(x_ref, images, 8)
    clear(xr_ref, 2 * classes, 8)

    loads[0].wait()
    ids = small_ref[cycles : cycles + 1, :images].astype(jnp.int32)
    onehot = (iota((LANES, images), 0) == ids).astype(F32)
    ctf = jnp.dot(small_ref[:cycles], onehot, precision=HP, preferred_element_type=F32)
    noise = column(small_ref[cycles + 1 : cycles + 2, :cycles])
    power = ctf * ctf / noise
    spread = (iota((cycles, LANES), 1) % SIDE == iota((cycles, LANES), 0)).astype(F32)
    weight = lax.dot_general(ctf / noise, spread, TN, precision=HP, preferred_element_type=F32)
    power_lanes = lax.dot_general(power, spread, TN, precision=HP, preferred_element_type=F32)
    shape = (depth * 8, cycles)
    row = iota(shape, 0)
    pick = ((row // 8) * share + row % 8 == iota(shape, 1)) & (row % 8 < share)
    by_dest = jnp.dot(pick.astype(F32), power, precision=HP, preferred_element_type=F32)
    by_dest = by_dest + (iota(by_dest.shape, 0) % 8 == share).astype(F32)
    log_prior = column(jnp.log(small_ref[cycles + 2 : cycles + 3, :classes]))

    eye = (iota((harm, harm), 0) == iota((harm, harm), 1)).astype(BF16)
    gap = jnp.zeros((SIDE - cycles, harm), BF16)

    def turn(first, second, ref, at0, at1):
        block = jnp.concatenate([first[0], gap, first[1], gap, second[0], gap, second[1], gap], axis=0)
        turned = lax.dot_general(eye, block, NT, preferred_element_type=F32)
        ref[pl.ds(at0 * STRIDE, harm), :] = turned[:, :LANES]
        ref[pl.ds(at1 * STRIDE, harm), :] = turned[:, LANES:]

    loads[1].wait()

    @pl.loop(0, classes, unroll=8)
    def _(c):
        real, imag = refs_ref[c, 0], refs_ref[c, 1]
        turn((real, imag), (imag, -real), xr_ref, c, classes + c)

    for n in range(PIECES):
        loads[2 + n].wait()

        @pl.loop(0, piece // 2, unroll=8)
        def _(pair):
            i = n * piece + pair * 2
            turn((image_ref[i, 0], image_ref[i, 1]), (image_ref[i + 1, 0], image_ref[i + 1, 1]), x_ref, i, i + 1)

    def one_residue(b, squares):
        image_parts, ref_parts = [], []
        for a in range(count):
            at = b + ROT * a
            x_part = (x_ref[pl.ds(at, images, stride=STRIDE), :] * weight).astype(BF16)
            r_part = xr_ref[pl.ds(at, 2 * classes, stride=STRIDE), :]
            squares = squares + r_part[:classes] * r_part[:classes]
            w_ref[b, :, a * LANES : (a + 1) * LANES] = x_part
            image_parts.append(x_part)
            ref_parts.append(r_part.astype(BF16))
        product = lax.dot_general(
            jnp.concatenate(image_parts, axis=1),
            jnp.concatenate(ref_parts, axis=1),
            NT,
            preferred_element_type=F32,
        )
        s_ref[b] = product.T
        return squares

    squares = lax.fori_loop(0, ROT, one_residue, jnp.zeros((classes, LANES), F32), unroll=12)
    model = lax.dot_general(squares, power_lanes, NT, precision=HP, preferred_element_type=F32)
    base = log_prior - 0.5 * model
    real = [s_ref[b, :classes] for b in range(ROT)]
    imag = [s_ref[b, classes:] for b in range(ROT)]
    even = [real[0]] + [real[b] + real[ROT - b] for b in range(1, HALF)] + [real[HALF]]
    odd = [None] + [imag[b] - imag[ROT - b] for b in range(1, HALF)]
    cosines, sines = half_transform(even, odd)
    score = [None] * ROT
    for k in range(HALF + 1):
        centre = cosines[k] + base
        if sines[k] is None:
            score[k] = centre
        else:
            score[k], score[ROT - k] = centre + sines[k], centre - sines[k]
    peak = score[0]
    for k in range(1, ROT):
        peak = jnp.maximum(peak, score[k])
    peak = jnp.max(peak, axis=0, keepdims=True)
    shifted = [jnp.exp(value - peak) for value in score]
    mass = shifted[0]
    for k in range(1, ROT):
        mass = mass + shifted[k]
    stats_ref[...] = jnp.zeros(stats_ref.shape, F32)
    stats_ref[0:1, 0:images] = peak
    stats_ref[1:2, 0:images] = jnp.sum(mass, axis=0, keepdims=True)

    pl.semaphore_wait(barrier, len(peers) + n_cls - 1)
    sends = []
    for j in range(1, n_cls):
        copy = pltpu.make_async_remote_copy(
            src_ref=stats_ref,
            dst_ref=gath_ref.at[j],
            send_sem=gath_send.at[j],
            recv_sem=gath_recv.at[j],
            device_id={"dp": dp, "cls": (cls + j) % n_cls},
            device_id_type=MESH,
        )
        copy.start()
        sends.append(copy)

    even = [shifted[0]] + [shifted[k] + shifted[ROT - k] for k in range(1, HALF)] + [shifted[HALF]]
    odd = [None] + [shifted[k] - shifted[ROT - k] for k in range(1, HALF)]
    cosines, sines = half_transform(even, odd)
    for b in range(HALF + 1):
        even_ref[b] = cosines[b]
        if sines[b] is not None:
            odd_ref[b] = sines[b]

    for copy in sends:
        copy.wait_recv()
    parts = [stats_ref[...]] + [gath_ref[j] for j in range(1, n_cls)]
    top = parts[0][0:1, :images]
    for part in parts[1:]:
        top = jnp.maximum(top, part[0:1, :images])
    total = jnp.zeros((1, images), F32)
    for part in parts:
        total = total + part[1:2, :images] * jnp.exp(part[0:1, :images] - top)
    evidence = top + jnp.log(total)
    evidence_ref[...] = evidence

    factor = jnp.exp(peak - evidence)
    mass = mass * factor
    for b in range(HALF + 1):
        real = (even_ref[b] * factor).astype(BF16)
        imag = jnp.zeros((classes, images), BF16) if sines[b] is None else (odd_ref[b] * factor).astype(BF16)
        back_ref[b] = jnp.concatenate([real, imag], axis=0)
        if 0 < b < HALF:
            back_ref[ROT - b] = jnp.concatenate([real, -imag], axis=0)
    den_ref[...] = jnp.zeros(den_ref.shape, F32)
    den_ref[:, 0:classes] = lax.dot_general(by_dest, mass, NT, precision=HP, preferred_element_type=F32)

    sign = jnp.where(iota((classes, LANES), 1) < SIDE, -1.0, 1.0)

    @pl.loop(0, ROT, unroll=12)
    def _(b):
        both = jnp.dot(back_ref[b], w_ref[b], preferred_element_type=F32)
        for a in range(count):
            part = both[:, a * LANES : (a + 1) * LANES]
            y_ref[pl.ds(b + ROT * a, classes, stride=STRIDE), :] = part[:classes] + sign * pltpu.roll(
                part[classes:], SIDE, 1
            )

    @pl.loop(0, classes, unroll=4)
    def _(c):
        for h in range(halves):
            t_ref[h, pl.ds(pl.multiple_of(c * LANES, LANES), LANES), :] = y_ref[
                pl.ds(c * STRIDE + h * LANES, LANES), :
            ].T

    def towards(node, source):
        ox, oz = parent[node][0] - node[0], parent[node][1] - node[1]
        return pltpu.make_async_remote_copy(
            src_ref=source,
            dst_ref=r_ref.at[index[node]],
            send_sem=tree_send.at[index[node]],
            recv_sem=tree_recv.at[index[node]],
            device_id={"dp": at_x(ox % 2) * depth + at_z(oz % depth), "cls": cls},
            device_id_type=MESH,
        )

    def assemble(dest):
        for p in range(2):
            for j in range(share):
                first = p * SIDE + dest * share + j
                for h in range(halves):
                    q = j * halves + h
                    l_ref[dest, p, q * classes : (q + 1) * classes, :] = t_ref[
                        h, pl.ds(first, classes, stride=LANES), :
                    ]
            l_ref[dest, p, blocks * classes :, :] = den_ref[pl.ds(pl.multiple_of(dest * 8, 8), 8), :]

    def gathered(node):
        value = l_ref[at_z(-node[1]), at_x(node[0])]
        for child in children[node]:
            towards(child, l_ref.at[0, 0]).wait_recv()
            value = value + r_ref[index[child]]
        return value

    assembled = []
    for node in parent:
        place = at_z(-node[1]), at_x(node[0])
        if node[1] not in assembled:
            assemble(place[0])
            assembled.append(node[1])
        if children[node]:
            l_ref[place] = gathered(node)
        towards(node, l_ref.at[place]).start()
    mine = gathered((0, 0))
    tail = mine[blocks * classes :, :]
    occ_ref[...] = tail[share : share + 1, 0:classes] * scale
    columns = jnp.concatenate([tail, jnp.zeros((LANES - 8, LANES), F32)], axis=0).T
    for j in range(share):
        below = columns[:classes, j : j + 1] + 1.0
        for h in range(halves):
            q = j * halves + h
            out_ref[:, q * LANES : (q + 1) * LANES] = mine[q * classes : (q + 1) * classes] / below
    for copy in sends:
        copy.wait_send()
    for node in parent:
        towards(node, l_ref.at[0, 0]).wait_send()


def shards(images, references, ctf_rows, group_ids, noise_var, class_prior):
    img_count, _, cycles, harm = images.shape
    classes = references.shape[0]
    n_dp, n_cls = lax.axis_size("dp"), lax.axis_size("cls")
    depth = n_dp // 2
    count = folds(harm)
    rows = count * ROT
    width = cycles // depth * harm
    chunk = width // LANES * classes + 8
    nodes = len(PARENT)
    def fitted(rows, above):
        return jnp.pad(rows, ((above, cycles + 8 - above - rows.shape[0]), (0, LANES - rows.shape[1])))

    small = (
        fitted(ctf_rows.T, 0)
        + fitted(group_ids.astype(F32).reshape(1, -1), cycles)
        + fitted(noise_var.reshape(1, -1), cycles + 1)
        + fitted(class_prior.reshape(1, -1), cycles + 2)
    )
    args = (images, references, small)
    new_references, occupancy, evidence = pl.pallas_call(
        functools.partial(kernel, classes * n_cls / (img_count * n_dp)),
        out_shape=[
            jax.ShapeDtypeStruct((classes, width), F32),
            jax.ShapeDtypeStruct((1, classes), F32),
            jax.ShapeDtypeStruct((1, img_count), F32),
        ],
        in_specs=[pl.BlockSpec(memory_space=pltpu.HBM)] * len(args),
        out_specs=[pl.BlockSpec(memory_space=pltpu.VMEM)] * 3,
        scratch_shapes=[
            *[pltpu.VMEM(arg.shape, arg.dtype) for arg in args],
            pltpu.VMEM((img_count * STRIDE, LANES), F32),
            pltpu.VMEM((2 * classes * STRIDE, LANES), F32),
            pltpu.VMEM((ROT, img_count, count * LANES), BF16),
            pltpu.VMEM((ROT, 2 * classes, img_count), F32),
            pltpu.VMEM((HALF + 1, classes, img_count), F32),
            pltpu.VMEM((HALF + 1, classes, img_count), F32),
            pltpu.VMEM((8, LANES), F32),
            pltpu.VMEM((n_cls, 8, LANES), F32),
            pltpu.VMEM((ROT, 2 * classes, img_count), BF16),
            pltpu.VMEM((classes * STRIDE, LANES), F32),
            pltpu.VMEM((harm // LANES, classes * LANES, LANES), F32),
            pltpu.VMEM((depth * 8, LANES), F32),
            pltpu.VMEM((depth, 2, chunk, LANES), F32),
            pltpu.VMEM((nodes, chunk, LANES), F32),
            pltpu.SemaphoreType.DMA((2 + PIECES,)),
            pltpu.SemaphoreType.DMA((n_cls,)),
            pltpu.SemaphoreType.DMA((n_cls,)),
            pltpu.SemaphoreType.DMA((nodes,)),
            pltpu.SemaphoreType.DMA((nodes,)),
        ],
        compiler_params=pltpu.CompilerParams(
            collective_id=0, has_side_effects=True, vmem_limit_bytes=107 * 2**19
        ),
    )(*args)
    return new_references, occupancy.reshape(-1), evidence.reshape(-1)


def solution(mesh):
    placed = (P("dp", None, None, None), P("cls", None, None, None), P(), P("dp"), P(), P("cls"))
    return jax.shard_map(
        shards,
        mesh=mesh,
        in_specs=placed,
        out_specs=(P("cls", "dp"), P("cls"), P("dp")),
        check_vma=False,
    )
```

```python
import functools
import math

import jax
import jax.numpy as jnp
from jax import lax
from jax.experimental import pallas as pl
from jax.experimental.pallas import tpu as pltpu
from jax.sharding import PartitionSpec as P

ROT = 36
HALF = ROT // 2
LANES = 128
SIDE = 64
HP = lax.Precision.HIGHEST
F32 = jnp.float32
BF16 = jnp.bfloat16
NT = (((1,), (1,)), ((), ()))
TN = (((0,), (0,)), ((), ()))
MESH = pl.DeviceIdType.MESH


def iota(shape, dim):
    return lax.broadcasted_iota(jnp.int32, shape, dim)


def half_transform(even, odd):
    quarter = HALF // 2
    even_sum = [even[b] + even[HALF - b] for b in range(quarter)]
    even_diff = [even[b] - even[HALF - b] for b in range(quarter)]
    odd_sum = [None] + [odd[b] + odd[HALF - b] for b in range(1, quarter)]
    odd_diff = [None] + [odd[b] - odd[HALF - b] for b in range(1, quarter)]
    cosines, sines = [], []
    for k in range(HALF + 1):
        source = even_sum if k % 2 == 0 else even_diff
        total = source[0]
        for b in range(1, quarter):
            total = total + source[b] * math.cos(math.pi * ((b * k) % ROT) / HALF)
        if k % 2 == 0:
            total = total + even[quarter] * (1.0 if k % 4 == 0 else -1.0)
        cosines.append(total)
    for k in range(HALF + 1):
        if k in (0, HALF):
            sines.append(None)
            continue
        source = odd_sum if k % 2 == 1 else odd_diff
        total = source[1] * math.sin(math.pi * k / HALF)
        for b in range(2, quarter):
            total = total + source[b] * math.sin(math.pi * ((b * k) % ROT) / HALF)
        if k % 2 == 1:
            total = total + odd[quarter] * (1.0 if k % 4 == 1 else -1.0)
        sines.append(total)
    return cosines, sines


def folds(harmonics):
    return -(-harmonics // ROT)


def column(row):
    square = (row.shape[1], row.shape[1])
    return jnp.sum(jnp.where(iota(square, 0) == iota(square, 1), row, 0.0), axis=1, keepdims=True)


PARENT = {
    (1, 7): (0, 7), (0, 8): (0, 7), (1, 8): (1, -7), (1, 6): (1, 5), (1, 3): (0, 3), (1, -5): (0, -5),
    (1, -3): (1, -2), (0, -7): (0, -6), (0, 5): (0, 4), (0, 7): (0, 6), (1, -7): (0, -6), (1, -6): (0, -6),
    (1, 5): (1, 4), (1, -2): (0, -2), (0, 3): (0, 2), (0, -5): (0, -4), (0, 6): (0, 4), (0, -3): (0, -2),
    (1, 2): (0, 2), (1, 4): (0, 4), (0, -6): (0, -4), (1, -4): (0, -4), (0, 2): (0, 1), (1, 0): (0, 0),
    (1, -1): (0, -1), (0, -2): (0, -1), (1, 1): (0, 1), (0, 4): (0, 0), (0, -4): (0, 0), (0, 1): (0, 0),
    (0, -1): (0, 0),
}
PIECES = 5
STRIDE = 289


def kernel(
    scale, image_hbm, refs_hbm, small_hbm,
    out_ref, occ_ref, evidence_ref,
    image_ref, refs_ref, small_ref,
    x_ref, xr_ref, w_ref, s_ref, even_ref, odd_ref, stats_ref, gath_ref, back_ref, y_ref, t_ref, den_ref, l_ref, r_ref,
    load_sem, gath_send, gath_recv, tree_send, tree_recv,
):
    images, _, cycles, harm = image_ref.shape
    classes = refs_ref.shape[0]
    count = folds(harm)
    rows = count * ROT
    depth = l_ref.shape[0]
    share = cycles // depth
    halves = harm // LANES
    blocks = share * halves
    piece = images // PIECES

    dp, cls = lax.axis_index("dp"), lax.axis_index("cls")
    n_cls = lax.axis_size("cls")
    x, z = dp // depth, dp % depth

    def at_z(step):
        return (z + step + depth) % depth

    def at_x(step):
        return (x + step) % 2

    ring = n_cls // 4

    def beside(j):
        return (
            (cls // (2 * ring) + j // (2 * ring)) % 2 * (2 * ring)
            + (cls // 2 % ring + j // 2 % ring) % ring * 2
            + (cls + j) % 2
        )

    def distance(j):
        y = j // 2 % ring
        return 2 * (j // (2 * ring)) + min(y, ring - y) + 0.1 * (j % 2)

    around = sorted(range(1, n_cls), key=distance, reverse=True)

    loads = [
        pltpu.make_async_copy(source, target, load_sem.at[n])
        for n, (source, target) in enumerate(
            [(small_hbm, small_ref), (refs_hbm, refs_ref)]
            + [(image_hbm.at[pl.ds(n * piece, piece)], image_ref.at[pl.ds(n * piece, piece)]) for n in range(PIECES)]
        )
    ]
    for load in loads:
        load.start()

    parent = PARENT
    index = {node: n for n, node in enumerate(parent)}
    children = {node: [other for other in parent if parent[other] == node] for node in [*parent, (0, 0)]}
    moves = {((parent[node][0] - node[0]) % 2, (parent[node][1] - node[1]) % depth) for node in parent}
    peers = sorted(moves | {(ox, -oz % depth) for ox, oz in moves})
    barrier = pltpu.get_barrier_semaphore()
    for ox, oz in peers:
        pl.semaphore_signal(
            barrier, inc=1, device_id={"dp": at_x(ox) * depth + at_z(oz), "cls": cls}, device_id_type=MESH
        )
    for j in around:
        pl.semaphore_signal(barrier, inc=1, device_id={"dp": dp, "cls": beside(j)}, device_id_type=MESH)

    def clear(ref, total, unroll):
        @pl.loop(0, total, unroll=unroll)
        def _(i):
            ref[pl.ds(i * STRIDE + harm, rows - harm), :] = jnp.zeros((rows - harm, LANES), F32)

    clear(x_ref, images, 8)
    clear(xr_ref, 2 * classes, 8)

    loads[0].wait()
    ids = small_ref[cycles : cycles + 1, :images].astype(jnp.int32)
    onehot = (iota((LANES, images), 0) == ids).astype(F32)
    ctf = jnp.dot(small_ref[:cycles], onehot, precision=HP, preferred_element_type=F32)
    noise = column(small_ref[cycles + 1 : cycles + 2, :cycles])
    power = ctf * ctf / noise
    spread = (iota((cycles, LANES), 1) % SIDE == iota((cycles, LANES), 0)).astype(F32)
    weight = lax.dot_general(ctf / noise, spread, TN, precision=HP, preferred_element_type=F32)
    power_lanes = lax.dot_general(power, spread, TN, precision=HP, preferred_element_type=F32)
    shape = (depth * 8, cycles)
    row = iota(shape, 0)
    pick = ((row // 8) * share + row % 8 == iota(shape, 1)) & (row % 8 < share)
    by_dest = jnp.dot(pick.astype(F32), power, precision=HP, preferred_element_type=F32)
    by_dest = by_dest + (iota(by_dest.shape, 0) % 8 == share).astype(F32)
    log_prior = column(jnp.log(small_ref[cycles + 2 : cycles + 3, :classes]))

    eye = (iota((harm, harm), 0) == iota((harm, harm), 1)).astype(BF16)
    gap = jnp.zeros((SIDE - cycles, harm), BF16)

    def turn(first, second, ref, at0, at1):
        block = jnp.concatenate([first[0], gap, first[1], gap, second[0], gap, second[1], gap], axis=0)
        turned = lax.dot_general(eye, block, NT, preferred_element_type=F32)
        ref[pl.ds(at0 * STRIDE, harm), :] = turned[:, :LANES]
        ref[pl.ds(at1 * STRIDE, harm), :] = turned[:, LANES:]

    loads[1].wait()

    @pl.loop(0, classes, unroll=16)
    def _(c):
        real, imag = refs_ref[c, 0], refs_ref[c, 1]
        turn((real, imag), (imag, -real), xr_ref, c, classes + c)

    for n in range(PIECES):
        loads[2 + n].wait()

        @pl.loop(0, piece // 2, unroll=8)
        def _(pair):
            i = n * piece + pair * 2
            turn((image_ref[i, 0], image_ref[i, 1]), (image_ref[i + 1, 0], image_ref[i + 1, 1]), x_ref, i, i + 1)

    def one_residue(b, squares):
        image_parts, ref_parts = [], []
        for a in range(count):
            at = b + ROT * a
            x_part = (x_ref[pl.ds(at, images, stride=STRIDE), :] * weight).astype(BF16)
            r_part = xr_ref[pl.ds(at, 2 * classes, stride=STRIDE), :]
            squares = squares + r_part[:classes] * r_part[:classes]
            w_ref[b, :, a * LANES : (a + 1) * LANES] = x_part
            image_parts.append(x_part)
            ref_parts.append(r_part.astype(BF16))
        product = lax.dot_general(
            jnp.concatenate(image_parts, axis=1),
            jnp.concatenate(ref_parts, axis=1),
            NT,
            preferred_element_type=F32,
        )
        s_ref[b] = product.T
        return squares

    squares = lax.fori_loop(0, ROT, one_residue, jnp.zeros((classes, LANES), F32), unroll=36)
    model = lax.dot_general(squares, power_lanes, NT, precision=HP, preferred_element_type=F32)
    base = log_prior - 0.5 * model
    real = [s_ref[b, :classes] for b in range(ROT)]
    imag = [s_ref[b, classes:] for b in range(ROT)]
    even = [real[0]] + [real[b] + real[ROT - b] for b in range(1, HALF)] + [real[HALF]]
    odd = [None] + [imag[b] - imag[ROT - b] for b in range(1, HALF)]
    cosines, sines = half_transform(even, odd)
    score = [None] * ROT
    for k in range(HALF + 1):
        centre = cosines[k] + base
        if sines[k] is None:
            score[k] = centre
        else:
            score[k], score[ROT - k] = centre + sines[k], centre - sines[k]
    peak = score[0]
    for k in range(1, ROT):
        peak = jnp.maximum(peak, score[k])
    peak = jnp.max(peak, axis=0, keepdims=True)
    shifted = [jnp.exp(value - peak) for value in score]
    mass = shifted[0]
    for k in range(1, ROT):
        mass = mass + shifted[k]
    stats_ref[...] = jnp.zeros(stats_ref.shape, F32)
    stats_ref[0:1, 0:images] = peak
    stats_ref[1:2, 0:images] = jnp.sum(mass, axis=0, keepdims=True)

    pl.semaphore_wait(barrier, len(peers) + n_cls - 1)
    sends = []
    for j in around:
        copy = pltpu.make_async_remote_copy(
            src_ref=stats_ref,
            dst_ref=gath_ref.at[j],
            send_sem=gath_send.at[j],
            recv_sem=gath_recv.at[j],
            device_id={"dp": dp, "cls": beside(j)},
            device_id_type=MESH,
        )
        copy.start()
        sends.append(copy)

    even = [shifted[0]] + [shifted[k] + shifted[ROT - k] for k in range(1, HALF)] + [shifted[HALF]]
    odd = [None] + [shifted[k] - shifted[ROT - k] for k in range(1, HALF)]
    cosines, sines = half_transform(even, odd)
    for b in range(HALF + 1):
        even_ref[b] = cosines[b]
        if sines[b] is not None:
            odd_ref[b] = sines[b]

    for copy in sends:
        copy.wait_recv()
    parts = [stats_ref[...]] + [gath_ref[j] for j in range(1, n_cls)]
    top = parts[0][0:1, :images]
    for part in parts[1:]:
        top = jnp.maximum(top, part[0:1, :images])
    total = jnp.zeros((1, images), F32)
    for part in parts:
        total = total + part[1:2, :images] * jnp.exp(part[0:1, :images] - top)
    evidence = top + jnp.log(total)
    evidence_ref[...] = evidence

    factor = jnp.exp(peak - evidence)
    mass = mass * factor
    for b in range(HALF + 1):
        real = (even_ref[b] * factor).astype(BF16)
        imag = jnp.zeros((classes, images), BF16) if sines[b] is None else (odd_ref[b] * factor).astype(BF16)
        back_ref[b] = jnp.concatenate([real, imag], axis=0)
        if 0 < b < HALF:
            back_ref[ROT - b] = jnp.concatenate([real, -imag], axis=0)
    den_ref[...] = jnp.zeros(den_ref.shape, F32)
    den_ref[:, 0:classes] = lax.dot_general(by_dest, mass, NT, precision=HP, preferred_element_type=F32)

    sign = jnp.where(iota((classes, LANES), 1) < SIDE, -1.0, 1.0)

    @pl.loop(0, ROT, unroll=36)
    def _(b):
        both = jnp.dot(back_ref[b], w_ref[b], preferred_element_type=F32)
        for a in range(count):
            part = both[:, a * LANES : (a + 1) * LANES]
            y_ref[pl.ds(b + ROT * a, classes, stride=STRIDE), :] = part[:classes] + sign * pltpu.roll(
                part[classes:], SIDE, 1
            )

    @pl.loop(0, classes, unroll=16)
    def _(c):
        for h in range(halves):
            t_ref[h, pl.ds(pl.multiple_of(c * LANES, LANES), LANES), :] = y_ref[
                pl.ds(c * STRIDE + h * LANES, LANES), :
            ].T

    def towards(node, source):
        ox, oz = parent[node][0] - node[0], parent[node][1] - node[1]
        return pltpu.make_async_remote_copy(
            src_ref=source,
            dst_ref=r_ref.at[index[node]],
            send_sem=tree_send.at[index[node]],
            recv_sem=tree_recv.at[index[node]],
            device_id={"dp": at_x(ox % 2) * depth + at_z(oz % depth), "cls": cls},
            device_id_type=MESH,
        )

    def assemble(dest):
        for p in range(2):
            for j in range(share):
                first = p * SIDE + dest * share + j
                for h in range(halves):
                    q = j * halves + h
                    l_ref[dest, p, q * classes : (q + 1) * classes, :] = t_ref[
                        h, pl.ds(first, classes, stride=LANES), :
                    ]
            l_ref[dest, p, blocks * classes :, :] = den_ref[pl.ds(pl.multiple_of(dest * 8, 8), 8), :]

    def gathered(node):
        value = l_ref[at_z(-node[1]), at_x(node[0])]
        for child in children[node]:
            towards(child, l_ref.at[0, 0]).wait_recv()
            value = value + r_ref[index[child]]
        return value

    assembled = []
    for node in parent:
        place = at_z(-node[1]), at_x(node[0])
        if node[1] not in assembled:
            assemble(place[0])
            assembled.append(node[1])
        if children[node]:
            l_ref[place] = gathered(node)
        towards(node, l_ref.at[place]).start()
    mine = gathered((0, 0))
    tail = mine[blocks * classes :, :]
    occ_ref[...] = tail[share : share + 1, 0:classes] * scale
    columns = jnp.concatenate([tail, jnp.zeros((LANES - 8, LANES), F32)], axis=0).T
    for j in range(share):
        below = columns[:classes, j : j + 1] + 1.0
        for h in range(halves):
            q = j * halves + h
            out_ref[:, q * LANES : (q + 1) * LANES] = mine[q * classes : (q + 1) * classes] / below
    for copy in sends:
        copy.wait_send()
    for node in parent:
        towards(node, l_ref.at[0, 0]).wait_send()


def shards(images, references, ctf_rows, group_ids, noise_var, class_prior):
    img_count, _, cycles, harm = images.shape
    classes = references.shape[0]
    n_dp, n_cls = lax.axis_size("dp"), lax.axis_size("cls")
    depth = n_dp // 2
    count = folds(harm)
    rows = count * ROT
    width = cycles // depth * harm
    chunk = width // LANES * classes + 8
    nodes = len(PARENT)
    def fitted(rows, above):
        return jnp.pad(rows, ((above, cycles + 8 - above - rows.shape[0]), (0, LANES - rows.shape[1])))

    small = (
        fitted(ctf_rows.T, 0)
        + fitted(group_ids.reshape(1, -1), cycles).astype(F32)
        + fitted(noise_var.reshape(1, -1), cycles + 1)
        + fitted(class_prior.reshape(1, -1), cycles + 2)
    )
    args = (images, references, small)
    new_references, occupancy, evidence = pl.pallas_call(
        functools.partial(kernel, classes * n_cls / (img_count * n_dp)),
        out_shape=[
            jax.ShapeDtypeStruct((classes, width), F32),
            jax.ShapeDtypeStruct((1, classes), F32),
            jax.ShapeDtypeStruct((1, img_count), F32),
        ],
        in_specs=[pl.BlockSpec(memory_space=pltpu.HBM)] * len(args),
        out_specs=[pl.BlockSpec(memory_space=pltpu.VMEM)] * 3,
        scratch_shapes=[
            *[pltpu.VMEM(arg.shape, arg.dtype) for arg in args],
            pltpu.VMEM((img_count * STRIDE, LANES), F32),
            pltpu.VMEM((2 * classes * STRIDE, LANES), F32),
            pltpu.VMEM((ROT, img_count, count * LANES), BF16),
            pltpu.VMEM((ROT, 2 * classes, img_count), F32),
            pltpu.VMEM((HALF + 1, classes, img_count), F32),
            pltpu.VMEM((HALF + 1, classes, img_count), F32),
            pltpu.VMEM((8, LANES), F32),
            pltpu.VMEM((n_cls, 8, LANES), F32),
            pltpu.VMEM((ROT, 2 * classes, img_count), BF16),
            pltpu.VMEM((classes * STRIDE, LANES), F32),
            pltpu.VMEM((harm // LANES, classes * LANES, LANES), F32),
            pltpu.VMEM((depth * 8, LANES), F32),
            pltpu.VMEM((depth, 2, chunk, LANES), F32),
            pltpu.VMEM((nodes, chunk, LANES), F32),
            pltpu.SemaphoreType.DMA((2 + PIECES,)),
            pltpu.SemaphoreType.DMA((n_cls,)),
            pltpu.SemaphoreType.DMA((n_cls,)),
            pltpu.SemaphoreType.DMA((nodes,)),
            pltpu.SemaphoreType.DMA((nodes,)),
        ],
        compiler_params=pltpu.CompilerParams(
            collective_id=0, has_side_effects=True, vmem_limit_bytes=107 * 2**19
        ),
    )(*args)
    return new_references, occupancy.reshape(-1), evidence.reshape(-1)


def solution(mesh):
    placed = (P("dp", None, None, None), P("cls", None, None, None), P(), P("dp"), P(), P("cls"))
    return jax.shard_map(
        shards,
        mesh=mesh,
        in_specs=placed,
        out_specs=(P("cls", "dp"), P("cls"), P("dp")),
        check_vma=False,
    )
```

```python
import functools
import math

import jax
import jax.numpy as jnp
from jax import lax
from jax.experimental import pallas as pl
from jax.experimental.pallas import tpu as pltpu
from jax.sharding import PartitionSpec as P

ROT = 36
HALF = ROT // 2
LANES = 128
SIDE = 64
HP = lax.Precision.HIGHEST
F32 = jnp.float32
BF16 = jnp.bfloat16
NT = (((1,), (1,)), ((), ()))
TN = (((0,), (0,)), ((), ()))
MESH = pl.DeviceIdType.MESH


def iota(shape, dim):
    return lax.broadcasted_iota(jnp.int32, shape, dim)


def half_transform(even, odd):
    quarter = HALF // 2
    even_sum = [even[b] + even[HALF - b] for b in range(quarter)]
    even_diff = [even[b] - even[HALF - b] for b in range(quarter)]
    odd_sum = [None] + [odd[b] + odd[HALF - b] for b in range(1, quarter)]
    odd_diff = [None] + [odd[b] - odd[HALF - b] for b in range(1, quarter)]
    cosines, sines = [], []
    for k in range(HALF + 1):
        source = even_sum if k % 2 == 0 else even_diff
        total = source[0]
        for b in range(1, quarter):
            total = total + source[b] * math.cos(math.pi * ((b * k) % ROT) / HALF)
        if k % 2 == 0:
            total = total + even[quarter] * (1.0 if k % 4 == 0 else -1.0)
        cosines.append(total)
    for k in range(HALF + 1):
        if k in (0, HALF):
            sines.append(None)
            continue
        source = odd_sum if k % 2 == 1 else odd_diff
        total = source[1] * math.sin(math.pi * k / HALF)
        for b in range(2, quarter):
            total = total + source[b] * math.sin(math.pi * ((b * k) % ROT) / HALF)
        if k % 2 == 1:
            total = total + odd[quarter] * (1.0 if k % 4 == 1 else -1.0)
        sines.append(total)
    return cosines, sines


def folds(harmonics):
    return -(-harmonics // ROT)


def column(row):
    square = (row.shape[1], row.shape[1])
    return jnp.sum(jnp.where(iota(square, 0) == iota(square, 1), row, 0.0), axis=1, keepdims=True)


PARENT = {
    (1, 7): (0, 7), (0, 8): (0, 7), (1, 8): (1, -7), (1, 6): (1, 5), (1, 3): (0, 3), (1, -5): (0, -5),
    (1, -3): (1, -2), (0, -7): (0, -6), (0, 5): (0, 4), (0, 7): (0, 6), (1, -7): (0, -6), (1, -6): (0, -6),
    (1, 5): (1, 4), (1, -2): (0, -2), (0, 3): (0, 2), (0, -5): (0, -4), (0, 6): (0, 4), (0, -3): (0, -2),
    (1, 2): (0, 2), (1, 4): (0, 4), (0, -6): (0, -4), (1, -4): (0, -4), (0, 2): (0, 1), (1, 0): (0, 0),
    (1, -1): (0, -1), (0, -2): (0, -1), (1, 1): (0, 1), (0, 4): (0, 0), (0, -4): (0, 0), (0, 1): (0, 0),
    (0, -1): (0, 0),
}
PIECES = 2
STRIDE = 289


def kernel(
    scale, image_hbm, refs_hbm, small_hbm,
    out_ref, occ_ref, evidence_ref,
    image_ref, refs_ref, small_ref,
    x_ref, xr_ref, w_ref, s_ref, even_ref, odd_ref, stats_ref, gath_ref, back_ref, y_ref, t_ref, den_ref, l_ref, r_ref,
    load_sem, gath_send, gath_recv, tree_send, tree_recv,
):
    images, _, cycles, harm = image_ref.shape
    classes = refs_ref.shape[0]
    count = folds(harm)
    rows = count * ROT
    depth = l_ref.shape[0]
    share = cycles // depth
    halves = harm // LANES
    blocks = share * halves
    piece = images // PIECES

    dp, cls = lax.axis_index("dp"), lax.axis_index("cls")
    n_cls = lax.axis_size("cls")
    x, z = dp // depth, dp % depth

    def at_z(step):
        return (z + step + depth) % depth

    def at_x(step):
        return (x + step) % 2

    ring = n_cls // 4

    def beside(j):
        return (
            (cls // (2 * ring) + j // (2 * ring)) % 2 * (2 * ring)
            + (cls // 2 % ring + j // 2 % ring) % ring * 2
            + (cls + j) % 2
        )

    def distance(j):
        y = j // 2 % ring
        return 2 * (j // (2 * ring)) + min(y, ring - y) + 0.1 * (j % 2)

    around = sorted(range(1, n_cls), key=distance, reverse=True)

    loads = [
        pltpu.make_async_copy(source, target, load_sem.at[n])
        for n, (source, target) in enumerate(
            [(small_hbm, small_ref), (refs_hbm, refs_ref)]
            + [(image_hbm.at[pl.ds(n * piece, piece)], image_ref.at[pl.ds(n * piece, piece)]) for n in range(PIECES)]
        )
    ]
    for load in loads:
        load.start()

    parent = PARENT
    index = {node: n for n, node in enumerate(parent)}
    children = {node: [other for other in parent if parent[other] == node] for node in [*parent, (0, 0)]}
    moves = {((parent[node][0] - node[0]) % 2, (parent[node][1] - node[1]) % depth) for node in parent}
    peers = sorted(moves | {(ox, -oz % depth) for ox, oz in moves})
    barrier = pltpu.get_barrier_semaphore()
    for ox, oz in peers:
        pl.semaphore_signal(
            barrier, inc=1, device_id={"dp": at_x(ox) * depth + at_z(oz), "cls": cls}, device_id_type=MESH
        )
    for j in around:
        pl.semaphore_signal(barrier, inc=1, device_id={"dp": dp, "cls": beside(j)}, device_id_type=MESH)

    def clear(ref, total, unroll):
        @pl.loop(0, total, unroll=unroll)
        def _(i):
            ref[pl.ds(i * STRIDE + harm, rows - harm), :] = jnp.zeros((rows - harm, LANES), F32)

    clear(x_ref, images, 8)
    clear(xr_ref, 2 * classes, 8)

    loads[0].wait()
    ids = small_ref[cycles : cycles + 1, :images].astype(jnp.int32)
    onehot = (iota((LANES, images), 0) == ids).astype(F32)
    ctf = jnp.dot(small_ref[:cycles], onehot, precision=HP, preferred_element_type=F32)
    noise = column(small_ref[cycles + 1 : cycles + 2, :cycles])
    power = ctf * ctf / noise
    spread = (iota((cycles, LANES), 1) % SIDE == iota((cycles, LANES), 0)).astype(F32)
    weight = lax.dot_general(ctf / noise, spread, TN, precision=HP, preferred_element_type=F32)
    power_lanes = lax.dot_general(power, spread, TN, precision=HP, preferred_element_type=F32)
    shape = (depth * 8, cycles)
    row = iota(shape, 0)
    pick = ((row // 8) * share + row % 8 == iota(shape, 1)) & (row % 8 < share)
    by_dest = jnp.dot(pick.astype(F32), power, precision=HP, preferred_element_type=F32)
    by_dest = by_dest + (iota(by_dest.shape, 0) % 8 == share).astype(F32)
    log_prior = column(jnp.log(small_ref[cycles + 2 : cycles + 3, :classes]))

    eye = (iota((harm, harm), 0) == iota((harm, harm), 1)).astype(BF16)
    gap = jnp.zeros((SIDE - cycles, harm), BF16)

    def turn(first, second, ref, at0, at1):
        block = jnp.concatenate([first[0], gap, first[1], gap, second[0], gap, second[1], gap], axis=0)
        turned = lax.dot_general(eye, block, NT, preferred_element_type=F32)
        ref[pl.ds(at0 * STRIDE, harm), :] = turned[:, :LANES]
        ref[pl.ds(at1 * STRIDE, harm), :] = turned[:, LANES:]

    loads[1].wait()

    @pl.loop(0, classes, unroll=16)
    def _(c):
        real, imag = refs_ref[c, 0], refs_ref[c, 1]
        turn((real, imag), (imag, -real), xr_ref, c, classes + c)

    for n in range(PIECES):
        loads[2 + n].wait()

        @pl.loop(0, piece // 2, unroll=20)
        def _(pair):
            i = n * piece + pair * 2
            turn((image_ref[i, 0], image_ref[i, 1]), (image_ref[i + 1, 0], image_ref[i + 1, 1]), x_ref, i, i + 1)

    def one_residue(b, squares):
        image_parts, ref_parts = [], []
        for a in range(count):
            at = b + ROT * a
            x_part = (x_ref[pl.ds(at, images, stride=STRIDE), :] * weight).astype(BF16)
            r_part = xr_ref[pl.ds(at, 2 * classes, stride=STRIDE), :]
            squares = squares + r_part[:classes] * r_part[:classes]
            w_ref[b, :, a * LANES : (a + 1) * LANES] = x_part
            image_parts.append(x_part)
            ref_parts.append(r_part.astype(BF16))
        product = lax.dot_general(
            jnp.concatenate(image_parts, axis=1),
            jnp.concatenate(ref_parts, axis=1),
            NT,
            preferred_element_type=F32,
        )
        s_ref[b] = product.T
        return squares

    squares = lax.fori_loop(0, ROT, one_residue, jnp.zeros((classes, LANES), F32), unroll=36)
    model = lax.dot_general(squares, power_lanes, NT, precision=HP, preferred_element_type=F32)
    base = log_prior - 0.5 * model
    real = [s_ref[b, :classes] for b in range(ROT)]
    imag = [s_ref[b, classes:] for b in range(ROT)]
    even = [real[0]] + [real[b] + real[ROT - b] for b in range(1, HALF)] + [real[HALF]]
    odd = [None] + [imag[b] - imag[ROT - b] for b in range(1, HALF)]
    cosines, sines = half_transform(even, odd)
    score = [None] * ROT
    for k in range(HALF + 1):
        centre = cosines[k] + base
        if sines[k] is None:
            score[k] = centre
        else:
            score[k], score[ROT - k] = centre + sines[k], centre - sines[k]
    peak = score[0]
    for k in range(1, ROT):
        peak = jnp.maximum(peak, score[k])
    peak = jnp.max(peak, axis=0, keepdims=True)
    shifted = [jnp.exp(value - peak) for value in score]
    mass = shifted[0]
    for k in range(1, ROT):
        mass = mass + shifted[k]
    stats_ref[...] = jnp.zeros(stats_ref.shape, F32)
    stats_ref[0:1, 0:images] = peak
    stats_ref[1:2, 0:images] = jnp.sum(mass, axis=0, keepdims=True)

    pl.semaphore_wait(barrier, len(peers) + n_cls - 1)
    sends = []
    for j in around:
        copy = pltpu.make_async_remote_copy(
            src_ref=stats_ref,
            dst_ref=gath_ref.at[j],
            send_sem=gath_send.at[j],
            recv_sem=gath_recv.at[j],
            device_id={"dp": dp, "cls": beside(j)},
            device_id_type=MESH,
        )
        copy.start()
        sends.append(copy)

    even = [shifted[0]] + [shifted[k] + shifted[ROT - k] for k in range(1, HALF)] + [shifted[HALF]]
    odd = [None] + [shifted[k] - shifted[ROT - k] for k in range(1, HALF)]
    cosines, sines = half_transform(even, odd)
    for b in range(HALF + 1):
        even_ref[b] = cosines[b]
        if sines[b] is not None:
            odd_ref[b] = sines[b]

    for copy in sends:
        copy.wait_recv()
    parts = [stats_ref[...]] + [gath_ref[j] for j in range(1, n_cls)]
    top = parts[0][0:1, :images]
    for part in parts[1:]:
        top = jnp.maximum(top, part[0:1, :images])
    total = jnp.zeros((1, images), F32)
    for part in parts:
        total = total + part[1:2, :images] * jnp.exp(part[0:1, :images] - top)
    evidence = top + jnp.log(total)
    evidence_ref[...] = evidence

    factor = jnp.exp(peak - evidence)
    mass = mass * factor
    for b in range(HALF + 1):
        real = (even_ref[b] * factor).astype(BF16)
        imag = jnp.zeros((classes, images), BF16) if sines[b] is None else (odd_ref[b] * factor).astype(BF16)
        back_ref[b] = jnp.concatenate([real, imag], axis=0)
        if 0 < b < HALF:
            back_ref[ROT - b] = jnp.concatenate([real, -imag], axis=0)
    den_ref[...] = jnp.zeros(den_ref.shape, F32)
    den_ref[:, 0:classes] = lax.dot_general(by_dest, mass, NT, precision=HP, preferred_element_type=F32)

    sign = jnp.where(iota((classes, LANES), 1) < SIDE, -1.0, 1.0)

    @pl.loop(0, ROT, unroll=36)
    def _(b):
        both = jnp.dot(back_ref[b], w_ref[b], preferred_element_type=F32)
        for a in range(count):
            part = both[:, a * LANES : (a + 1) * LANES]
            y_ref[pl.ds(b + ROT * a, classes, stride=STRIDE), :] = part[:classes] + sign * pltpu.roll(
                part[classes:], SIDE, 1
            )

    @pl.loop(0, classes, unroll=16)
    def _(c):
        for h in range(halves):
            t_ref[h, pl.ds(pl.multiple_of(c * LANES, LANES), LANES), :] = y_ref[
                pl.ds(c * STRIDE + h * LANES, LANES), :
            ].T

    def towards(node, source):
        ox, oz = parent[node][0] - node[0], parent[node][1] - node[1]
        return pltpu.make_async_remote_copy(
            src_ref=source,
            dst_ref=r_ref.at[index[node]],
            send_sem=tree_send.at[index[node]],
            recv_sem=tree_recv.at[index[node]],
            device_id={"dp": at_x(ox % 2) * depth + at_z(oz % depth), "cls": cls},
            device_id_type=MESH,
        )

    def assemble(dest):
        for p in range(2):
            for j in range(share):
                first = p * SIDE + dest * share + j
                for h in range(halves):
                    q = j * halves + h
                    l_ref[dest, p, q * classes : (q + 1) * classes, :] = t_ref[
                        h, pl.ds(first, classes, stride=LANES), :
                    ]
            l_ref[dest, p, blocks * classes :, :] = den_ref[pl.ds(pl.multiple_of(dest * 8, 8), 8), :]

    def gathered(node):
        value = l_ref[at_z(-node[1]), at_x(node[0])]
        for child in children[node]:
            towards(child, l_ref.at[0, 0]).wait_recv()
            value = value + r_ref[index[child]]
        return value

    assembled = []
    for node in parent:
        place = at_z(-node[1]), at_x(node[0])
        if node[1] not in assembled:
            assemble(place[0])
            assembled.append(node[1])
        if children[node]:
            l_ref[place] = gathered(node)
        towards(node, l_ref.at[place]).start()
    mine = gathered((0, 0))
    tail = mine[blocks * classes :, :]
    occ_ref[...] = tail[share : share + 1, 0:classes] * scale
    columns = jnp.concatenate([tail, jnp.zeros((LANES - 8, LANES), F32)], axis=0).T
    for j in range(share):
        below = columns[:classes, j : j + 1] + 1.0
        for h in range(halves):
            q = j * halves + h
            out_ref[:, q * LANES : (q + 1) * LANES] = mine[q * classes : (q + 1) * classes] / below
    for copy in sends:
        copy.wait_send()
    for node in parent:
        towards(node, l_ref.at[0, 0]).wait_send()


def shards(images, references, ctf_rows, group_ids, noise_var, class_prior):
    img_count, _, cycles, harm = images.shape
    classes = references.shape[0]
    n_dp, n_cls = lax.axis_size("dp"), lax.axis_size("cls")
    depth = n_dp // 2
    count = folds(harm)
    rows = count * ROT
    width = cycles // depth * harm
    chunk = width // LANES * classes + 8
    nodes = len(PARENT)
    def fitted(rows, above):
        return jnp.pad(rows, ((above, cycles + 8 - above - rows.shape[0]), (0, LANES - rows.shape[1])))

    small = (
        fitted(ctf_rows.T, 0)
        + fitted(group_ids.reshape(1, -1), cycles).astype(F32)
        + fitted(noise_var.reshape(1, -1), cycles + 1)
        + fitted(class_prior.reshape(1, -1), cycles + 2)
    )
    args = (images, references, small)
    new_references, occupancy, evidence = pl.pallas_call(
        functools.partial(kernel, classes * n_cls / (img_count * n_dp)),
        out_shape=[
            jax.ShapeDtypeStruct((classes, width), F32),
            jax.ShapeDtypeStruct((1, classes), F32),
            jax.ShapeDtypeStruct((1, img_count), F32),
        ],
        in_specs=[pl.BlockSpec(memory_space=pltpu.HBM)] * len(args),
        out_specs=[pl.BlockSpec(memory_space=pltpu.VMEM)] * 3,
        scratch_shapes=[
            *[pltpu.VMEM(arg.shape, arg.dtype) for arg in args],
            pltpu.VMEM((img_count * STRIDE, LANES), F32),
            pltpu.VMEM((2 * classes * STRIDE, LANES), F32),
            pltpu.VMEM((ROT, img_count, count * LANES), BF16),
            pltpu.VMEM((ROT, 2 * classes, img_count), F32),
            pltpu.VMEM((HALF + 1, classes, img_count), F32),
            pltpu.VMEM((HALF + 1, classes, img_count), F32),
            pltpu.VMEM((8, LANES), F32),
            pltpu.VMEM((n_cls, 8, LANES), F32),
            pltpu.VMEM((ROT, 2 * classes, img_count), BF16),
            pltpu.VMEM((classes * STRIDE, LANES), F32),
            pltpu.VMEM((harm // LANES, classes * LANES, LANES), F32),
            pltpu.VMEM((depth * 8, LANES), F32),
            pltpu.VMEM((depth, 2, chunk, LANES), F32),
            pltpu.VMEM((nodes, chunk, LANES), F32),
            pltpu.SemaphoreType.DMA((2 + PIECES,)),
            pltpu.SemaphoreType.DMA((n_cls,)),
            pltpu.SemaphoreType.DMA((n_cls,)),
            pltpu.SemaphoreType.DMA((nodes,)),
            pltpu.SemaphoreType.DMA((nodes,)),
        ],
        compiler_params=pltpu.CompilerParams(
            collective_id=0, has_side_effects=True, vmem_limit_bytes=107 * 2**19
        ),
    )(*args)
    return new_references, occupancy.reshape(-1), evidence.reshape(-1)


def solution(mesh):
    placed = (P("dp", None, None, None), P("cls", None, None, None), P(), P("dp"), P(), P("cls"))
    return jax.shard_map(
        shards,
        mesh=mesh,
        in_specs=placed,
        out_specs=(P("cls", "dp"), P("cls"), P("dp")),
        check_vma=False,
    )
```

```python
import functools
import math

import jax
import jax.numpy as jnp
from jax import lax
from jax.experimental import pallas as pl
from jax.experimental.pallas import tpu as pltpu
from jax.sharding import PartitionSpec as P

ROT = 36
HALF = ROT // 2
LANES = 128
SIDE = 64
HP = lax.Precision.HIGHEST
F32 = jnp.float32
BF16 = jnp.bfloat16
NT = (((1,), (1,)), ((), ()))
TN = (((0,), (0,)), ((), ()))
MESH = pl.DeviceIdType.MESH


def iota(shape, dim):
    return lax.broadcasted_iota(jnp.int32, shape, dim)


def half_transform(even, odd):
    quarter = HALF // 2
    even_sum = [even[b] + even[HALF - b] for b in range(quarter)]
    even_diff = [even[b] - even[HALF - b] for b in range(quarter)]
    odd_sum = [None] + [odd[b] + odd[HALF - b] for b in range(1, quarter)]
    odd_diff = [None] + [odd[b] - odd[HALF - b] for b in range(1, quarter)]
    cosines, sines = [], []
    for k in range(HALF + 1):
        source = even_sum if k % 2 == 0 else even_diff
        total = source[0]
        for b in range(1, quarter):
            total = total + source[b] * math.cos(math.pi * ((b * k) % ROT) / HALF)
        if k % 2 == 0:
            total = total + even[quarter] * (1.0 if k % 4 == 0 else -1.0)
        cosines.append(total)
    for k in range(HALF + 1):
        if k in (0, HALF):
            sines.append(None)
            continue
        source = odd_sum if k % 2 == 1 else odd_diff
        total = source[1] * math.sin(math.pi * k / HALF)
        for b in range(2, quarter):
            total = total + source[b] * math.sin(math.pi * ((b * k) % ROT) / HALF)
        if k % 2 == 1:
            total = total + odd[quarter] * (1.0 if k % 4 == 1 else -1.0)
        sines.append(total)
    return cosines, sines


def folds(harmonics):
    return -(-harmonics // ROT)


def column(row):
    square = (row.shape[1], row.shape[1])
    return jnp.sum(jnp.where(iota(square, 0) == iota(square, 1), row, 0.0), axis=1, keepdims=True)


PARENT = {
    (1, 7): (0, 7), (0, 8): (0, 7), (1, 8): (1, -7), (1, 6): (1, 5), (1, 3): (0, 3), (1, -5): (0, -5),
    (1, -3): (1, -2), (0, -7): (0, -6), (0, 5): (0, 4), (0, 7): (0, 6), (1, -7): (0, -6), (1, -6): (0, -6),
    (1, 5): (1, 4), (1, -2): (0, -2), (0, 3): (0, 2), (0, -5): (0, -4), (0, 6): (0, 4), (0, -3): (0, -2),
    (1, 2): (0, 2), (1, 4): (0, 4), (0, -6): (0, -4), (1, -4): (0, -4), (0, 2): (0, 1), (1, 0): (0, 0),
    (1, -1): (0, -1), (0, -2): (0, -1), (1, 1): (0, 1), (0, 4): (0, 0), (0, -4): (0, 0), (0, 1): (0, 0),
    (0, -1): (0, 0),
}
PIECES = 2
STRIDE = 289


def kernel(
    scale, image_hbm, refs_hbm, small_hbm,
    out_ref, occ_ref, evidence_ref,
    image_ref, refs_ref, small_ref,
    x_ref, xr_ref, w_ref, s_ref, even_ref, odd_ref, stats_ref, gath_ref, back_ref, y_ref, t_ref, den_ref, l_ref, r_ref,
    load_sem, gath_send, gath_recv, tree_send, tree_recv,
):
    images, _, cycles, harm = image_ref.shape
    classes = refs_ref.shape[0]
    count = folds(harm)
    rows = count * ROT
    depth = l_ref.shape[0]
    share = cycles // depth
    halves = harm // LANES
    blocks = share * halves
    piece = images // PIECES

    dp, cls = lax.axis_index("dp"), lax.axis_index("cls")
    n_cls = lax.axis_size("cls")
    x, z = dp // depth, dp % depth

    def at_z(step):
        return (z + step + depth) % depth

    def at_x(step):
        return (x + step) % 2

    ring = n_cls // 4

    def beside(j):
        return (
            (cls // (2 * ring) + j // (2 * ring)) % 2 * (2 * ring)
            + (cls // 2 % ring + j // 2 % ring) % ring * 2
            + (cls + j) % 2
        )

    def distance(j):
        y = j // 2 % ring
        return 2 * (j // (2 * ring)) + min(y, ring - y) + 0.1 * (j % 2)

    around = sorted(range(1, n_cls), key=distance, reverse=True)

    loads = [
        pltpu.make_async_copy(source, target, load_sem.at[n])
        for n, (source, target) in enumerate(
            [(small_hbm, small_ref), (refs_hbm, refs_ref)]
            + [(image_hbm.at[pl.ds(n * piece, piece)], image_ref.at[pl.ds(n * piece, piece)]) for n in range(PIECES)]
        )
    ]
    for load in loads:
        load.start()

    parent = PARENT
    index = {node: n for n, node in enumerate(parent)}
    children = {node: [other for other in parent if parent[other] == node] for node in [*parent, (0, 0)]}
    moves = {((parent[node][0] - node[0]) % 2, (parent[node][1] - node[1]) % depth) for node in parent}
    peers = sorted(moves | {(ox, -oz % depth) for ox, oz in moves})
    barrier = pltpu.get_barrier_semaphore()
    for ox, oz in peers:
        pl.semaphore_signal(
            barrier, inc=1, device_id={"dp": at_x(ox) * depth + at_z(oz), "cls": cls}, device_id_type=MESH
        )
    for j in around:
        pl.semaphore_signal(barrier, inc=1, device_id={"dp": dp, "cls": beside(j)}, device_id_type=MESH)

    def clear(ref, total, unroll):
        @pl.loop(0, total, unroll=unroll)
        def _(i):
            ref[pl.ds(i * STRIDE + harm, rows - harm), :] = jnp.zeros((rows - harm, LANES), F32)

    clear(x_ref, images, 8)
    clear(xr_ref, 2 * classes, 8)

    loads[0].wait()
    ids = small_ref[cycles : cycles + 1, :images].astype(jnp.int32)
    onehot = (iota((LANES, images), 0) == ids).astype(F32)
    ctf = jnp.dot(small_ref[:cycles], onehot, precision=HP, preferred_element_type=F32)
    noise = column(small_ref[cycles + 1 : cycles + 2, :cycles])
    power = ctf * ctf / noise
    spread = (iota((cycles, LANES), 1) % SIDE == iota((cycles, LANES), 0)).astype(F32)
    weight = lax.dot_general(ctf / noise, spread, TN, precision=HP, preferred_element_type=F32)
    power_lanes = lax.dot_general(power, spread, TN, precision=HP, preferred_element_type=F32)
    shape = (depth * 8, cycles)
    row = iota(shape, 0)
    pick = ((row // 8) * share + row % 8 == iota(shape, 1)) & (row % 8 < share)
    by_dest = jnp.dot(pick.astype(F32), power, precision=HP, preferred_element_type=F32)
    by_dest = by_dest + (iota(by_dest.shape, 0) % 8 == share).astype(F32)
    log_prior = column(jnp.log(small_ref[cycles + 2 : cycles + 3, :classes]))

    eye = (iota((harm, harm), 0) == iota((harm, harm), 1)).astype(BF16)
    gap = jnp.zeros((SIDE - cycles, harm), BF16)

    def turn(first, second, ref, at0, at1):
        block = jnp.concatenate([first[0], gap, first[1], gap, second[0], gap, second[1], gap], axis=0)
        turned = lax.dot_general(eye, block, NT, preferred_element_type=F32)
        ref[pl.ds(at0 * STRIDE, harm), :] = turned[:, :LANES]
        ref[pl.ds(at1 * STRIDE, harm), :] = turned[:, LANES:]

    loads[1].wait()

    @pl.loop(0, classes, unroll=16)
    def _(c):
        real, imag = refs_ref[c, 0], refs_ref[c, 1]
        turn((real, imag), (imag, -real), xr_ref, c, classes + c)

    for n in range(PIECES):
        loads[2 + n].wait()

        @pl.loop(0, piece // 10, unroll=piece // 10)
        def _(group):
            i = n * piece + group * 10
            for at in (i, i + 2):
                turn((image_ref[at, 0], image_ref[at, 1]), (image_ref[at + 1, 0], image_ref[at + 1, 1]), x_ref, at, at + 1)
            for step in range(4, 10):
                block = jnp.concatenate([image_ref[i + step, 0], gap, image_ref[i + step, 1], gap], axis=0)
                x_ref[pl.ds((i + step) * STRIDE, harm), :] = block.astype(F32).T

    def one_residue(b, squares):
        image_parts, ref_parts = [], []
        for a in range(count):
            at = b + ROT * a
            x_part = (x_ref[pl.ds(at, images, stride=STRIDE), :] * weight).astype(BF16)
            r_part = xr_ref[pl.ds(at, 2 * classes, stride=STRIDE), :]
            squares = squares + r_part[:classes] * r_part[:classes]
            w_ref[b, :, a * LANES : (a + 1) * LANES] = x_part
            image_parts.append(x_part)
            ref_parts.append(r_part.astype(BF16))
        product = lax.dot_general(
            jnp.concatenate(image_parts, axis=1),
            jnp.concatenate(ref_parts, axis=1),
            NT,
            preferred_element_type=F32,
        )
        s_ref[b] = product.T
        return squares

    squares = lax.fori_loop(0, ROT, one_residue, jnp.zeros((classes, LANES), F32), unroll=36)
    model = lax.dot_general(squares, power_lanes, NT, precision=HP, preferred_element_type=F32)
    base = log_prior - 0.5 * model
    real = [s_ref[b, :classes] for b in range(ROT)]
    imag = [s_ref[b, classes:] for b in range(ROT)]
    even = [real[0]] + [real[b] + real[ROT - b] for b in range(1, HALF)] + [real[HALF]]
    odd = [None] + [imag[b] - imag[ROT - b] for b in range(1, HALF)]
    cosines, sines = half_transform(even, odd)
    score = [None] * ROT
    for k in range(HALF + 1):
        centre = cosines[k] + base
        if sines[k] is None:
            score[k] = centre
        else:
            score[k], score[ROT - k] = centre + sines[k], centre - sines[k]
    peak = score[0]
    for k in range(1, ROT):
        peak = jnp.maximum(peak, score[k])
    peak = jnp.max(peak, axis=0, keepdims=True)
    shifted = [jnp.exp(value - peak) for value in score]
    mass = shifted[0]
    for k in range(1, ROT):
        mass = mass + shifted[k]
    stats_ref[...] = jnp.zeros(stats_ref.shape, F32)
    stats_ref[0:1, 0:images] = peak
    stats_ref[1:2, 0:images] = jnp.sum(mass, axis=0, keepdims=True)

    pl.semaphore_wait(barrier, len(peers) + n_cls - 1)
    sends = []
    for j in around:
        copy = pltpu.make_async_remote_copy(
            src_ref=stats_ref,
            dst_ref=gath_ref.at[j],
            send_sem=gath_send.at[j],
            recv_sem=gath_recv.at[j],
            device_id={"dp": dp, "cls": beside(j)},
            device_id_type=MESH,
        )
        copy.start()
        sends.append(copy)

    even = [shifted[0]] + [shifted[k] + shifted[ROT - k] for k in range(1, HALF)] + [shifted[HALF]]
    odd = [None] + [shifted[k] - shifted[ROT - k] for k in range(1, HALF)]
    cosines, sines = half_transform(even, odd)
    for b in range(HALF + 1):
        even_ref[b] = cosines[b]
        if sines[b] is not None:
            odd_ref[b] = sines[b]

    for copy in sends:
        copy.wait_recv()
    parts = [stats_ref[...]] + [gath_ref[j] for j in range(1, n_cls)]
    top = parts[0][0:1, :images]
    for part in parts[1:]:
        top = jnp.maximum(top, part[0:1, :images])
    total = jnp.zeros((1, images), F32)
    for part in parts:
        total = total + part[1:2, :images] * jnp.exp(part[0:1, :images] - top)
    evidence = top + jnp.log(total)
    evidence_ref[...] = evidence

    factor = jnp.exp(peak - evidence)
    mass = mass * factor
    for b in range(HALF + 1):
        real = (even_ref[b] * factor).astype(BF16)
        imag = jnp.zeros((classes, images), BF16) if sines[b] is None else (odd_ref[b] * factor).astype(BF16)
        back_ref[b] = jnp.concatenate([real, imag], axis=0)
        if 0 < b < HALF:
            back_ref[ROT - b] = jnp.concatenate([real, -imag], axis=0)
    den_ref[...] = jnp.zeros(den_ref.shape, F32)
    den_ref[:, 0:classes] = lax.dot_general(by_dest, mass, NT, precision=HP, preferred_element_type=F32)

    sign = jnp.where(iota((classes, LANES), 1) < SIDE, -1.0, 1.0)

    @pl.loop(0, ROT, unroll=36)
    def _(b):
        both = jnp.dot(back_ref[b], w_ref[b], preferred_element_type=F32)
        for a in range(count):
            part = both[:, a * LANES : (a + 1) * LANES]
            y_ref[pl.ds(b + ROT * a, classes, stride=STRIDE), :] = part[:classes] + sign * pltpu.roll(
                part[classes:], SIDE, 1
            )

    @pl.loop(0, classes, unroll=16)
    def _(c):
        for h in range(halves):
            t_ref[h, pl.ds(pl.multiple_of(c * LANES, LANES), LANES), :] = y_ref[
                pl.ds(c * STRIDE + h * LANES, LANES), :
            ].T

    def towards(node, source):
        ox, oz = parent[node][0] - node[0], parent[node][1] - node[1]
        return pltpu.make_async_remote_copy(
            src_ref=source,
            dst_ref=r_ref.at[index[node]],
            send_sem=tree_send.at[index[node]],
            recv_sem=tree_recv.at[index[node]],
            device_id={"dp": at_x(ox % 2) * depth + at_z(oz % depth), "cls": cls},
            device_id_type=MESH,
        )

    def assemble(dest):
        for p in range(2):
            for j in range(share):
                first = p * SIDE + dest * share + j
                for h in range(halves):
                    q = j * halves + h
                    l_ref[dest, p, q * classes : (q + 1) * classes, :] = t_ref[
                        h, pl.ds(first, classes, stride=LANES), :
                    ]
            l_ref[dest, p, blocks * classes :, :] = den_ref[pl.ds(pl.multiple_of(dest * 8, 8), 8), :]

    def gathered(node):
        value = l_ref[at_z(-node[1]), at_x(node[0])]
        for child in children[node]:
            towards(child, l_ref.at[0, 0]).wait_recv()
            value = value + r_ref[index[child]]
        return value

    assembled = []
    for node in parent:
        place = at_z(-node[1]), at_x(node[0])
        if node[1] not in assembled:
            assemble(place[0])
            assembled.append(node[1])
        if children[node]:
            l_ref[place] = gathered(node)
        towards(node, l_ref.at[place]).start()
    mine = gathered((0, 0))
    tail = mine[blocks * classes :, :]
    occ_ref[...] = tail[share : share + 1, 0:classes] * scale
    columns = jnp.concatenate([tail, jnp.zeros((LANES - 8, LANES), F32)], axis=0).T
    for j in range(share):
        below = columns[:classes, j : j + 1] + 1.0
        for h in range(halves):
            q = j * halves + h
            out_ref[:, q * LANES : (q + 1) * LANES] = mine[q * classes : (q + 1) * classes] / below
    for copy in sends:
        copy.wait_send()
    for node in parent:
        towards(node, l_ref.at[0, 0]).wait_send()


def shards(images, references, ctf_rows, group_ids, noise_var, class_prior):
    img_count, _, cycles, harm = images.shape
    classes = references.shape[0]
    n_dp, n_cls = lax.axis_size("dp"), lax.axis_size("cls")
    depth = n_dp // 2
    count = folds(harm)
    rows = count * ROT
    width = cycles // depth * harm
    chunk = width // LANES * classes + 8
    nodes = len(PARENT)
    def fitted(rows, above):
        return jnp.pad(rows, ((above, cycles + 8 - above - rows.shape[0]), (0, LANES - rows.shape[1])))

    small = (
        fitted(ctf_rows.T, 0)
        + fitted(group_ids.reshape(1, -1), cycles).astype(F32)
        + fitted(noise_var.reshape(1, -1), cycles + 1)
        + fitted(class_prior.reshape(1, -1), cycles + 2)
    )
    args = (images, references, small)
    new_references, occupancy, evidence = pl.pallas_call(
        functools.partial(kernel, classes * n_cls / (img_count * n_dp)),
        out_shape=[
            jax.ShapeDtypeStruct((classes, width), F32),
            jax.ShapeDtypeStruct((1, classes), F32),
            jax.ShapeDtypeStruct((1, img_count), F32),
        ],
        in_specs=[pl.BlockSpec(memory_space=pltpu.HBM)] * len(args),
        out_specs=[pl.BlockSpec(memory_space=pltpu.VMEM)] * 3,
        scratch_shapes=[
            *[pltpu.VMEM(arg.shape, arg.dtype) for arg in args],
            pltpu.VMEM((img_count * STRIDE, LANES), F32),
            pltpu.VMEM((2 * classes * STRIDE, LANES), F32),
            pltpu.VMEM((ROT, img_count, count * LANES), BF16),
            pltpu.VMEM((ROT, 2 * classes, img_count), F32),
            pltpu.VMEM((HALF + 1, classes, img_count), F32),
            pltpu.VMEM((HALF + 1, classes, img_count), F32),
            pltpu.VMEM((8, LANES), F32),
            pltpu.VMEM((n_cls, 8, LANES), F32),
            pltpu.VMEM((ROT, 2 * classes, img_count), BF16),
            pltpu.VMEM((classes * STRIDE, LANES), F32),
            pltpu.VMEM((harm // LANES, classes * LANES, LANES), F32),
            pltpu.VMEM((depth * 8, LANES), F32),
            pltpu.VMEM((depth, 2, chunk, LANES), F32),
            pltpu.VMEM((nodes, chunk, LANES), F32),
            pltpu.SemaphoreType.DMA((2 + PIECES,)),
            pltpu.SemaphoreType.DMA((n_cls,)),
            pltpu.SemaphoreType.DMA((n_cls,)),
            pltpu.SemaphoreType.DMA((nodes,)),
            pltpu.SemaphoreType.DMA((nodes,)),
        ],
        compiler_params=pltpu.CompilerParams(
            collective_id=0, has_side_effects=True, vmem_limit_bytes=107 * 2**19
        ),
    )(*args)
    return new_references, occupancy.reshape(-1), evidence.reshape(-1)


def solution(mesh):
    placed = (P("dp", None, None, None), P("cls", None, None, None), P(), P("dp"), P(), P("cls"))
    return jax.shard_map(
        shards,
        mesh=mesh,
        in_specs=placed,
        out_specs=(P("cls", "dp"), P("cls"), P("dp")),
        check_vma=False,
    )
```
